32 devices in a mesh: run: 2 (over core), ctx: 4 (over z), head: 4 (over y, x).
Axes of the slice: x: 2, y: 2, z: 4, core: 2. Of those that a mesh axis runs over, the one named last changes fastest.
Arguments:
- inner_tokens: bfloat16 [16384, 5120], P(('run', 'ctx', 'head')), parts along dimension 0, may hold values from -6 to 6
- state_inputs: bfloat16 [16384, 256], P(('run', 'ctx', 'head')), parts along dimension 0, may hold values from -6 to 6
- step_raw: bfloat16 [16384, 80], P(('run', 'ctx', 'head')), parts along dimension 0, may hold values from -3 to 24
- conv_inner: float32 [5, 5120], P(None, 'head'), may hold values from -3 to 3
- conv_state: float32 [5, 256], replicated, may hold values from -3 to 3
- head_rates: float32 [4, 80], P('run', 'head'), parts along dimension 0, may hold values from -15 to 4
- skip_gain: float32 [80], P('head'), may hold values from 0.5 to 1.5
Outputs:
- mixed: bfloat16 [16384, 5120], P(('run', 'ctx', 'head')), parts along dimension 0
The draws below stay inside these ranges and needn't reach their ends.
There are 2 independent parts, one for each index of `run`. The reference program is written for one: setup_inputs(seed, part) draws one part's arguments, and reference() takes and returns one part's arrays. A program takes and returns all parts, laid end to end along the dimension named above; an argument that names none is the same for every part. Nothing has to cross between parts.
All inputs are finite; a program needn't handle non-finite values.
Results may differ from the reference program's by a relative error of at most 0.009.
Values may be sent and summed in bfloat16 or wider, within the bound.
A program may use at most 192 MiB of HBM per device.

```python
import jax
import jax.numpy as jnp
from jax import lax

HEADS = 80
HEAD_DIM = 64
STATE = 128
KERNEL = 4
SPAN = 256
INNER = 5120
SEQ = 8192


def head_profile(key):
    first, second, third = jax.random.split(jax.random.fold_in(key, 17), 3)
    share = 0.5
    quick = jax.random.bernoulli(first, share, (HEADS,))
    jitter_step = jax.random.uniform(second, (HEADS,), jnp.float32, 0.5, 2.0)
    jitter_rate = jax.random.uniform(third, (HEADS,), jnp.float32, 0.6, 1.6)
    quick_step = 0.003 * jitter_step
    slow_step = 3.0 / SEQ * jitter_step
    chosen_step = jnp.where(quick, quick_step, slow_step)
    quick_rate = 0.025 / quick_step * jitter_rate
    slow_rate = 0.4 / (SEQ * slow_step) * jitter_rate
    selected_rate = jnp.where(quick, quick_rate, slow_rate)
    return (quick, chosen_step, selected_rate)


def draw_head_rates(key, part):
    quick, chosen_step, selected_rate = head_profile(key)
    row_bias_vector = jnp.log(jnp.expm1(chosen_step))
    return jnp.stack([row_bias_vector, jnp.log(selected_rate)], axis=0).astype(jnp.float32)


def draw_step_raw(key, part):
    quick, chosen_step, selected_rate = head_profile(key)
    row_bias_vector = jnp.log(jnp.expm1(chosen_step))
    noise_key, block_key, offset_key, gap_key, loss_key = jax.random.split(jax.random.fold_in(key, 29), 5)
    base = 0.5 * jax.random.truncated_normal(noise_key, -6.0, 6.0, (SEQ, HEADS), jnp.float32)
    positions = jnp.arange(SEQ, dtype=jnp.int32)[:, None]
    block_start = jax.random.randint(block_key, (2, HEADS), 0, SEQ // SPAN) * SPAN
    first_place = block_start + jax.random.randint(offset_key, (2, HEADS), 0, SPAN // 2)
    second_place = first_place + jax.random.randint(gap_key, (2, HEADS), 1, SPAN // 2 + 1)
    dropped_flags = jax.random.uniform(loss_key, (4, HEADS), jnp.float32, 0.22, 0.4)
    places = jnp.concatenate([first_place, second_place], axis=0)
    bursty = jnp.logical_not(quick)
    unscaled_values = base
    for selector_index in range(4):
        spike_value = jnp.log(jnp.expm1(dropped_flags[selector_index] / selected_rate)) - row_bias_vector
        event_mask = jnp.logical_and(positions == places[selector_index][None, :], bursty[None, :])
        unscaled_values = jnp.where(event_mask, spike_value[None, :], unscaled_values)
    return unscaled_values.astype(jnp.bfloat16)


def segment_offsets(key):
    segment_count = SEQ // 64 + 1
    shared_key, other_key, mapping_key = jax.random.split(jax.random.fold_in(key, 41), 3)
    shared = jax.random.uniform(shared_key, (segment_count, STATE), jnp.float32, -2.0, 2.0)
    c_offsets = jax.random.uniform(other_key, (segment_count, STATE), jnp.float32, -2.0, 2.0)
    head_keys = jax.random.split(mapping_key, HEADS)
    mapping = jax.vmap(lambda single: jax.random.permutation(single, STATE)[:HEAD_DIM])(head_keys).reshape(HEADS * HEAD_DIM).astype(jnp.int32)
    segment = (jnp.arange(SEQ, dtype=jnp.int32) // 64).astype(jnp.int32)
    return (shared, c_offsets, mapping, segment)


def token_noise(key, columns):
    return jax.random.truncated_normal(key, -4.0, 4.0, (SEQ, columns), jnp.float32)


def draw_inner_tokens(key, part):
    shared, c_offsets, mapping, segment = segment_offsets(key)
    noise = token_noise(jax.random.fold_in(key, 53), HEADS * HEAD_DIM)
    per_segment = jnp.take(shared, mapping, axis=1)
    per_token = jnp.take(per_segment, segment, axis=0)
    return jnp.clip(noise + per_token, -6.0, 6.0).astype(jnp.bfloat16)


def draw_state_inputs(key, part):
    shared, c_offsets, mapping, segment = segment_offsets(key)
    noise = token_noise(jax.random.fold_in(key, 59), 2 * STATE)
    offsets = jnp.concatenate([jnp.take(shared, segment, axis=0), jnp.take(c_offsets, segment, axis=0)], axis=1)
    return jnp.clip(noise + offsets, -6.0, 6.0).astype(jnp.bfloat16)


def shard_levels(rng, shape, cuts, low, high):
    level = 1.0
    for axis_at, parts in cuts:
        heights = jax.random.uniform(jax.random.fold_in(jax.random.fold_in(rng, 6), axis_at), (parts,), jnp.float32, low / len(cuts), high / len(cuts))
        level = level * jnp.repeat(jnp.exp(heights), shape[axis_at] // parts).reshape((-1,) + (1,) * (len(shape) - 1 - axis_at))
    return level


def centred(key, extent, scale, reach, cuts=(), kind=jnp.bfloat16):
    loudness = shard_levels(key, extent, cuts, -0.22, 0.18) if cuts else 1.0
    drawn = jax.random.normal(key, extent, jnp.float32) * scale * loudness
    return jnp.minimum(jnp.maximum(drawn, -reach), reach).astype(kind)


def setup_inputs(seed: int = 0, part: int = 0) -> dict:
    arg_keys = jax.random.split(jax.random.key(seed), 8)
    part_splits = jax.random.split(jax.random.fold_in(arg_keys[7], part), 8)
    return {
        "inner_tokens": draw_inner_tokens(jax.random.fold_in(jax.random.fold_in(arg_keys[7], part), 71), part),
        "state_inputs": draw_state_inputs(jax.random.fold_in(jax.random.fold_in(arg_keys[7], part), 71), part),
        "step_raw": draw_step_raw(jax.random.fold_in(jax.random.fold_in(arg_keys[7], part), 71), part),
        "conv_inner": centred(arg_keys[3], (KERNEL + 1, INNER), 0.5, 3.0, ((1, 4),), jnp.float32),
        "conv_state": centred(arg_keys[4], (KERNEL + 1, 2 * STATE), 0.5, 3.0, (), jnp.float32),
        "head_rates": draw_head_rates(jax.random.fold_in(jax.random.fold_in(arg_keys[7], part), 71), part),
        "skip_gain": jnp.clip(0.5 + 1.0 * jax.random.uniform(arg_keys[6], (HEADS,), jnp.float32) ** shard_levels(arg_keys[6], (HEADS,), ((0, 4),), -0.2, 0.2), 0.5, 1.5),
    }


def silu_conv(signal, kernel_taps):
    length = signal.shape[0]
    channels = signal.shape[1]
    padded = jnp.concatenate([jnp.zeros((KERNEL - 1, channels), jnp.float32), signal.astype(jnp.float32)], axis=0)
    summed = jnp.zeros((length, channels), jnp.float32) + kernel_taps[KERNEL][None, :]
    for offset in range(KERNEL):
        summed = summed + kernel_taps[offset][None, :] * padded[offset:offset + length]
    return jax.nn.silu(summed).astype(jnp.bfloat16)


def block_terms(carry_state, pieces):
    c_block, b_block, u_block, decay_block = pieces
    cumulative = jnp.cumsum(decay_block, axis=0)
    across = cumulative.T
    inner_scores = jnp.dot(c_block, b_block.T, preferred_element_type=jnp.float32)
    spread = across[:, :, None] - across[:, None, :]
    places = jnp.arange(c_block.shape[0])
    causal = places[:, None] >= places[None, :]
    mixing = (inner_scores[None] * jnp.exp(jnp.where(causal[None], spread, -jnp.inf))).astype(jnp.bfloat16)
    local_terms = jnp.einsum("hts,shp->thp", mixing.astype(jnp.float32), u_block.astype(jnp.float32), precision=lax.Precision.HIGHEST)
    carried = jnp.exp(cumulative)[:, :, None] * jnp.einsum("tn,hpn->thp", c_block.astype(jnp.float32), carry_state, precision=lax.Precision.HIGHEST)
    ending = cumulative[-1]
    weights = jnp.exp(ending[None, :] - cumulative)
    scaled = weights[:, :, None] * u_block.astype(jnp.float32)
    new_state = jnp.exp(ending)[:, None, None] * carry_state + jnp.einsum("shp,sn->hpn", scaled, b_block.astype(jnp.float32), precision=lax.Precision.HIGHEST)
    return new_state, local_terms + carried


def reference(inner_tokens, state_inputs, step_raw, conv_inner, conv_state, head_rates, skip_gain):
    inner_conv = silu_conv(inner_tokens, conv_inner)
    state_conv = silu_conv(state_inputs, conv_state)
    b_rows = state_conv[:, :STATE]
    c_rows = state_conv[:, STATE:]
    step_size = jax.nn.softplus(step_raw.astype(jnp.float32) + head_rates[0][None, :])
    log_decay = -step_size * jnp.exp(head_rates[1])[None, :]
    x_heads = inner_conv.reshape(SEQ, HEADS, HEAD_DIM).astype(jnp.float32)
    inputs = (x_heads * step_size[:, :, None]).astype(jnp.bfloat16)
    block_count = SEQ // SPAN
    start_state = jnp.zeros((HEADS, HEAD_DIM, STATE), jnp.float32)
    final_state, outputs = lax.scan(block_terms, start_state, (c_rows.reshape(block_count, SPAN, STATE), b_rows.reshape(block_count, SPAN, STATE), inputs.reshape(block_count, SPAN, HEADS, HEAD_DIM), log_decay.reshape(block_count, SPAN, HEADS)))
    summed = outputs.reshape(SEQ, HEADS, HEAD_DIM) + skip_gain[None, :, None] * x_heads
    return summed.astype(jnp.bfloat16).reshape(SEQ, INNER)
```

```python
import functools

import jax
import jax.numpy as jnp
from jax import lax
from jax.experimental import pallas as pl
from jax.experimental.pallas import tpu as pltpu
from jax.sharding import PartitionSpec as P

KERNEL = 4
SPAN = 256
GROUP = 256
LANES = 128
LOG2E = 1.4426950408889634
F32 = jnp.float32
BF16 = jnp.bfloat16
MESH = pl.DeviceIdType.MESH


def dot(a, b):
    return jnp.dot(a, b, preferred_element_type=F32)


def split2(v):
    hi = v.astype(BF16)
    lo = (v - hi.astype(F32)).astype(BF16)
    return jnp.concatenate([hi, lo], axis=1)


def silu(v):
    return v * (0.5 + 0.5 * jnp.tanh(0.5 * v))


def softplus(v):
    return jnp.maximum(v, 0.0) + jnp.log(1.0 + jnp.exp(-jnp.abs(v)))


def kernel(
    n_ctx, n_head, heads, width, pieces,
    x_ref, si_ref, sr_ref, cw_ref, cs_ref, sm_ref, out_ref,
    cwb, smb, eb32, ebs, ebr, edge, sedge, xs,
    cum, cum_t, step_hl, w_hl, ec_hl, dec_hl, scores, bt, cc,
    xc, acc, s0, dx, s_out, slots, d_slots, qs, rs, ch_in, ch_out, p_out, inc,
    cw_ss, cw_rs, sm_ss, sm_rs, eb_ss, eb_rs, s_ss, s_rs, d_ss, d_rs, ch_ss, ch_rs, p_ss, p_rs,
):
    tokens, channels = x_ref.shape
    blocks = tokens // SPAN
    per = GROUP // width
    state = cc.shape[1]
    run = lax.axis_index("run")
    c = lax.axis_index("ctx")
    me = lax.axis_index("head")
    flat = c * n_head + me
    total = n_ctx * n_head
    nxt = lax.rem(flat + 1, total)
    prv = lax.rem(flat + total - 1, total)
    up = lax.rem(c + 1, n_ctx)
    down = lax.rem(c + n_ctx - 1, n_ctx)

    def peer(i):
        return lax.rem(me + i, n_head)

    def at_head(h):
        return (run, c, h)

    barrier = pltpu.get_barrier_semaphore()
    for i in range(1, n_head):
        pl.semaphore_signal(barrier, inc=1, device_id=at_head(peer(i)), device_id_type=MESH)
    for f in (nxt, prv):
        pl.semaphore_signal(
            barrier, inc=1, device_id=(run, f // n_head, lax.rem(f, n_head)), device_id_type=MESH
        )
    for z in (up, down):
        pl.semaphore_signal(barrier, inc=1, device_id=(run, z, me), device_id_type=MESH)

    part = channels // 5
    tail = x_ref[tokens - 16:, :].astype(F32)
    stail = si_ref[tokens - 16:, :].astype(F32)
    eb32[...] = jnp.zeros_like(eb32)
    for i in range(5):
        eb32[3 * i:3 * i + 3, :] = tail[13:16, i * part:(i + 1) * part]
    for r in range(3):
        eb32[15:16, r * 2 * state:(r + 1) * 2 * state] = stail[13 + r:14 + r, :]
    ebs[...] = eb32[...].astype(BF16)
    cwb[me] = cw_ref[...]
    smb[me] = pltpu.roll(sm_ref[...], me * (heads // n_head), 1)

    pl.semaphore_wait(barrier, n_head - 1 + 4)

    edge_copy = pltpu.make_async_remote_copy(
        ebs, ebr, eb_ss, eb_rs, device_id=(run, nxt // n_head, lax.rem(nxt, n_head)), device_id_type=MESH
    )
    edge_copy.start()

    def param_copies(dst, slot, k):
        return (
            pltpu.make_async_remote_copy(
                smb.at[slot], smb.at[slot], sm_ss.at[k], sm_rs.at[slot],
                device_id=at_head(dst), device_id_type=MESH),
            pltpu.make_async_remote_copy(
                cwb.at[slot], cwb.at[slot], cw_ss.at[k], cw_rs.at[slot],
                device_id=at_head(dst), device_id_type=MESH),
        )

    for i in range(1, n_head):
        for copy in param_copies(peer(i), me, i):
            copy.start()
    for i in range(1, n_head):
        param_copies(peer(i), peer(i), i)[0].wait_recv()

    small = jnp.sum(smb[...], axis=0)
    bias = small[0:1]
    rate = jnp.exp(small[1:2])
    gain = small[2:3]
    raw = jnp.concatenate(
        [sr_ref[...].astype(F32), jnp.zeros((tokens, LANES - heads), F32)], axis=1
    )
    step = softplus(raw + bias)
    decay = -step * rate
    rows = lax.broadcasted_iota(jnp.int32, (SPAN, SPAN), 0)
    cols = lax.broadcasted_iota(jnp.int32, (SPAN, SPAN), 1)
    lower = rows >= cols
    tri = jnp.where(lower, 1.0, 0.0).astype(F32)
    step_hl[...] = split2(step)
    ends = []
    for b in range(blocks):
        lo = b * SPAN
        cm = jnp.dot(tri, decay[lo:lo + SPAN] * LOG2E, precision=lax.Precision.HIGHEST,
                     preferred_element_type=F32)
        cum[lo:lo + SPAN, :] = cm
        cum_t[:, lo:lo + SPAN] = cm.T
        end = cm[SPAN - 1:SPAN]
        w_hl[lo:lo + SPAN, :] = split2(jnp.exp2(end - cm))
        ec_hl[lo:lo + SPAN, :] = split2(jnp.exp2(cm))
        ends.append(end)
    dec_rows = jnp.concatenate(
        [jnp.exp2(ends[0]), jnp.exp2(ends[1]), jnp.exp2(ends[0] + ends[1]), gain,
         jnp.zeros((12, LANES), F32)], axis=0)
    dec_hl[...] = split2(dec_rows)

    edge_copy.wait_recv()
    eb32[...] = jnp.where(flat == 0, 0.0, ebr[...].astype(F32))
    for i in range(5):
        edge[5:8, i * part:(i + 1) * part] = eb32[3 * i:3 * i + 3, :]
    for r in range(3):
        sedge[5 + r:6 + r, :] = eb32[15:16, r * 2 * state:(r + 1) * 2 * state]

    def conv(l, taps):
        v = taps(KERNEL) + taps(0) * xs[l, pl.ds(8 - KERNEL + 1, tokens), :]
        for k in range(1, KERNEL):
            v = v + taps(k) * xs[l, pl.ds(8 - KERNEL + 1 + k, tokens), :]
        return silu(v).astype(BF16)

    for l in range(2):
        at = pl.ds(l * LANES, LANES)
        xs[l, 0:8, :] = sedge[:, at]
        xs[l, 8:8 + tokens, :] = si_ref[:, at].astype(F32)
    b_conv = conv(0, lambda k: cs_ref[k:k + 1, 0:LANES])
    c_conv = conv(1, lambda k: cs_ref[k:k + 1, LANES:2 * LANES])
    b_t = b_conv.astype(F32).T.astype(BF16)
    bt[...] = b_t
    cc[...] = c_conv
    for b in range(blocks):
        lo = b * SPAN
        sc = dot(c_conv[lo:lo + SPAN], b_t[:, lo:lo + SPAN])
        scores[b] = jnp.where(lower, sc, 0.0)

    for i in range(1, n_head):
        param_copies(peer(i), peer(i), i)[1].wait_recv()

    def spreader(g):
        k = lax.broadcasted_iota(jnp.int32, (2 * LANES, GROUP), 0)
        l = lax.broadcasted_iota(jnp.int32, (2 * LANES, GROUP), 1)
        return jnp.where(lax.rem(k, LANES) == g * per + l // width, 1.0, 0.0).astype(BF16)

    def state_copies(dst, slot, k, j):
        return (
            pltpu.make_async_remote_copy(
                s_out.at[dst, j], slots.at[slot, j], s_ss.at[k, j], s_rs.at[slot, j],
                device_id=at_head(dst), device_id_type=MESH),
            pltpu.make_async_remote_copy(
                dx.at[dst, j], d_slots.at[slot, j], d_ss.at[k, j], d_rs.at[slot, j],
                device_id=at_head(dst), device_id_type=MESH),
        )

    def form(q, j):
        g = q * pieces + j
        base = pl.multiple_of(g * GROUP, GROUP)
        jb = pl.multiple_of(j * GROUP, GROUP)
        spread = spreader(g)
        us = []
        sb = dot(step_hl[...], spread)
        wb = dot(w_hl[...], spread)
        for l in range(2):
            at = pl.ds(pl.multiple_of(base + l * LANES, LANES), LANES)
            tap_at = pl.ds(pl.multiple_of(jb + l * LANES, LANES), LANES)
            xs[l, 0:8, :] = edge[:, at]
            xs[l, 8:8 + tokens, :] = x_ref[:, at].astype(F32)
            xv = conv(l, lambda k: cwb[q, k:k + 1, tap_at])
            xc[:, at] = xv
            half = slice(l * LANES, (l + 1) * LANES)
            u = (xv.astype(F32) * sb[:, half]).astype(BF16)
            us.append((u.astype(F32) * wb[:, half]).astype(BF16))
        uw = jnp.concatenate(us, axis=1)
        d = dot(dec_hl[...], spread)[0:8]
        dx[q, j] = d
        first = dot(bt[:, 0:SPAN], uw[0:SPAN])
        second = dot(bt[:, SPAN:2 * SPAN], uw[SPAN:2 * SPAN])
        s0[q, j] = first
        s_out[q, j] = (d[1:2] * first + second).astype(BF16)

    def form_piece(j, carry):
        def far(i, carry2):
            q = peer(i)
            form(q, j)
            for copy in state_copies(q, me, i, j):
                copy.start()
            return carry2

        lax.fori_loop(1, n_head, far, 0)
        form(me, j)
        slots[me, j] = s_out[me, j]
        d_slots[me, j] = dx[me, j]
        return carry

    lax.fori_loop(0, pieces, form_piece, 0)

    lane = lax.broadcasted_iota(jnp.int32, (1, LANES), 1)

    def local(g, b):
        lo = b * SPAN
        half = SPAN // 2
        base = pl.multiple_of(g * GROUP, GROUP)
        q = g // pieces
        j = lax.rem(g, pieces)
        spread = spreader(g)
        sb = dot(step_hl[lo:lo + SPAN, :], spread)
        turned = pltpu.roll(cum[lo:lo + SPAN, :], lax.rem(LANES - g * per, LANES), 1)
        top_scores = scores[b, 0:half, 0:half]
        low_scores = scores[b, half:SPAN, :]
        for l in range(2):
            at = pl.ds(pl.multiple_of(base + l * LANES, LANES), LANES)
            xv = xc[lo:lo + SPAN, at].astype(F32)
            u = (xv * sb[:, l * LANES:(l + 1) * LANES]).astype(BF16)
            tops, lows = [], []
            for k in range(2):
                h = l * 2 + k
                col = turned[:, h:h + 1]
                row = cum_t[pl.ds(g * per + h, 1), lo:lo + SPAN]
                top = jnp.exp2(jnp.minimum(col[0:half] - row[:, 0:half], 0.0)) * top_scores
                low = jnp.exp2(jnp.minimum(col[half:SPAN] - row, 0.0)) * low_scores
                tops.append(dot(top.astype(BF16), u[0:half]))
                lows.append(dot(low.astype(BF16), u))
            skip = dx[q, j, 3:4, l * LANES:(l + 1) * LANES]
            acc[lo:lo + half, at] = (
                jnp.where(lane < width, tops[0], tops[1]) + skip * xv[0:half])
            acc[lo + half:lo + SPAN, at] = (
                jnp.where(lane < width, lows[0], lows[1]) + skip * xv[half:SPAN])

    def local_all(b):
        def body(g, carry):
            local(g, b)
            return carry
        lax.fori_loop(0, n_head * pieces, body, 0)

    local_all(0)

    def chain_copy(j):
        return pltpu.make_async_remote_copy(
            ch_out.at[j], ch_in.at[j], ch_ss.at[j], ch_rs.at[j],
            device_id=(run, up, me), device_id_type=MESH)

    def gather_piece(j, carry):
        for i in range(1, n_head):
            for copy in state_copies(peer(i), peer(i), i, j):
                copy.wait_recv()
        q_sum = slots[0, j].astype(F32)
        r = d_slots[0, j, 2:3]
        for e in range(1, n_head):
            d = d_slots[e, j, 2:3]
            q_sum = d * q_sum + slots[e, j].astype(F32)
            r = d * r
        qs[j] = q_sum
        rs[j] = jnp.broadcast_to(r, (8, GROUP))
        return carry

    lax.fori_loop(0, pieces, gather_piece, 0)

    def back_copy(dst, slot, k, j):
        return pltpu.make_async_remote_copy(
            p_out.at[dst, j], inc.at[slot, j], p_ss.at[k, j], p_rs.at[slot, j],
            device_id=at_head(dst), device_id_type=MESH)

    def chain_piece(j, carry):
        @pl.when(c > 0)
        def _():
            chain_copy(j).wait_recv()

        @pl.when(c == 0)
        def _():
            ch_in[j] = jnp.zeros((state, GROUP), BF16)

        arriving = ch_in[j].astype(F32)

        @pl.when(c < n_ctx - 1)
        def _():
            ch_out[j] = (rs[j, 0:1] * arriving + qs[j]).astype(BF16)
            chain_copy(j).start()

        prefix = arriving
        p_out[0, j] = prefix.astype(BF16)
        for e in range(1, n_head):
            prefix = d_slots[e - 1, j, 2:3] * prefix + slots[e - 1, j].astype(F32)
            p_out[e, j] = prefix.astype(BF16)
        for i in range(1, n_head):
            back_copy(peer(i), me, i, j).start()
        inc[me, j] = p_out[me, j]
        return carry

    lax.fori_loop(0, pieces, chain_piece, 0)

    local_all(1)

    def finish(q, j):
        g = q * pieces + j
        base = pl.multiple_of(g * GROUP, GROUP)
        spread = spreader(g)
        entering = inc[q, j]
        middle = (dx[q, j, 0:1] * entering.astype(F32) + s0[q, j]).astype(BF16)
        eb = dot(ec_hl[...], spread)
        at = pl.ds(base, GROUP)
        out_ref[0:SPAN, at] = (
            acc[0:SPAN, at] + eb[0:SPAN] * dot(cc[0:SPAN, :], entering)).astype(BF16)
        out_ref[SPAN:2 * SPAN, at] = (
            acc[SPAN:2 * SPAN, at] + eb[SPAN:2 * SPAN] * dot(cc[SPAN:2 * SPAN, :], middle)
        ).astype(BF16)

    def finish_piece(j, carry):
        finish(me, j)

        def far(i, carry2):
            q = peer(i)
            back_copy(q, q, i, j).wait_recv()
            finish(q, j)
            return carry2

        return lax.fori_loop(1, n_head, far, carry)

    lax.fori_loop(0, pieces, finish_piece, 0)

    edge_copy.wait_send()
    for i in range(1, n_head):
        for copy in param_copies(peer(i), me, i):
            copy.wait_send()

    def drain(j, carry):
        for i in range(1, n_head):
            for copy in state_copies(peer(i), me, i, j):
                copy.wait_send()
            back_copy(peer(i), me, i, j).wait_send()

        @pl.when(c < n_ctx - 1)
        def _():
            chain_copy(j).wait_send()
        return carry

    lax.fori_loop(0, pieces, drain, 0)


def per_device(n_ctx, n_head, inner_tokens, state_inputs, step_raw, conv_inner, conv_state, head_rates, skip_gain):
    tokens, channels = inner_tokens.shape
    heads = step_raw.shape[1]
    width = channels // heads
    state = state_inputs.shape[1] // 2
    pieces = channels // n_head // GROUP
    taps = conv_inner.shape[0]
    cw = jnp.pad(conv_inner, ((0, 8 - taps), (0, 0)))
    small = jnp.concatenate([head_rates, skip_gain[None]], axis=0)
    small = jnp.pad(small, ((0, 8 - small.shape[0]), (0, LANES - small.shape[1])))
    part = channels // n_head
    vm = pltpu.VMEM
    dma = pltpu.SemaphoreType.DMA
    grid4 = (n_head, pieces, state, GROUP)
    scratch = [
        vm((n_head, 8, part), F32), vm((n_head, 8, LANES), F32),
        vm((16, channels // 5), F32), vm((16, channels // 5), BF16), vm((16, channels // 5), BF16),
        vm((8, channels), F32), vm((8, 2 * state), F32), vm((2, tokens + 8, LANES), F32),
        vm((tokens, LANES), F32), vm((LANES, tokens), F32),
        vm((tokens, 2 * LANES), BF16), vm((tokens, 2 * LANES), BF16), vm((tokens, 2 * LANES), BF16),
        vm((16, 2 * LANES), BF16),
        vm((tokens // SPAN, SPAN, SPAN), F32), vm((state, tokens), BF16), vm((tokens, state), BF16),
        vm((tokens, channels), BF16), vm((tokens, channels), F32),
        vm(grid4, F32), vm((n_head, pieces, 8, GROUP), F32),
        vm(grid4, BF16), vm(grid4, BF16), vm((n_head, pieces, 8, GROUP), F32),
        vm((pieces, state, GROUP), F32), vm((pieces, 8, GROUP), F32),
        vm((pieces, state, GROUP), BF16), vm((pieces, state, GROUP), BF16),
        vm(grid4, BF16), vm(grid4, BF16),
        dma((n_head,)), dma((n_head,)), dma((n_head,)), dma((n_head,)),
        dma, dma,
        dma((n_head, pieces)), dma((n_head, pieces)), dma((n_head, pieces)), dma((n_head, pieces)),
        dma((pieces,)), dma((pieces,)),
        dma((n_head, pieces)), dma((n_head, pieces)),
    ]
    return pl.pallas_call(
        functools.partial(kernel, n_ctx, n_head, heads, width, pieces),
        out_shape=jax.ShapeDtypeStruct((tokens, channels), BF16),
        in_specs=[pl.BlockSpec(memory_space=pltpu.VMEM)] * 6,
        out_specs=pl.BlockSpec(memory_space=pltpu.VMEM),
        scratch_shapes=scratch,
        compiler_params=pltpu.CompilerParams(
            collective_id=0, has_side_effects=True, vmem_limit_bytes=60 * 1024 * 1024
        ),
        name="ssd_layer",
    )(inner_tokens, state_inputs, step_raw, cw, conv_state, small)


def solution(mesh):
    return jax.shard_map(
        functools.partial(per_device, mesh.shape["ctx"], mesh.shape["head"]),
        mesh=mesh,
        in_specs=(
            P(("run", "ctx", "head"), None),
            P(("run", "ctx", "head"), None),
            P(("run", "ctx", "head"), None),
            P(None, "head"),
            P(),
            P("run", "head"),
            P("head"),
        ),
        out_specs=P(("run", "ctx", "head"), None),
        check_vma=False,
    )
```

```python
import functools

import jax
import jax.numpy as jnp
from jax import lax
from jax.experimental import pallas as pl
from jax.experimental.pallas import tpu as pltpu
from jax.sharding import PartitionSpec as P

KERNEL = 4
SPAN = 256
GROUP = 256
LANES = 128
LOG2E = 1.4426950408889634
F32 = jnp.float32
BF16 = jnp.bfloat16
MESH = pl.DeviceIdType.MESH


def dot(a, b):
    return jnp.dot(a, b, preferred_element_type=F32)


def split2(v):
    hi = v.astype(BF16)
    lo = (v - hi.astype(F32)).astype(BF16)
    return jnp.concatenate([hi, lo], axis=1)


def silu(v):
    return v * (0.5 + 0.5 * jnp.tanh(0.5 * v))


def softplus(v):
    return jnp.maximum(v, 0.0) + jnp.log(1.0 + jnp.exp(-jnp.abs(v)))


def kernel(
    n_ctx, n_head, heads, width, pieces,
    x_hbm, si_ref, sr_ref, cw_ref, cs_ref, hr_ref, sg_ref,
    acc_hbm, inc, s0_hbm, dx, ec_hl, cc,
    x_ref, tail_v, cwb, smb, eb32, ebs, ebr, edge, sedge, xs,
    cum, cum_t, step_hl, w_hl, dec_hl, scores, bt,
    xc, uv, acc, s0, s_out, slots, d_slots, ch_in, ch_out, p_out,
    cw_ss, cw_rs, sm_ss, sm_rs, eb_ss, eb_rs, s_ss, s_rs, d_ss, d_rs, ch_ss, ch_rs, p_ss, p_rs,
    x_sem, tail_sem, acc_sem, s0_sem, own_sem,
):
    tokens, channels = x_ref.shape
    blocks = tokens // SPAN
    per = GROUP // width
    state = cc.shape[1]
    run = lax.axis_index("run")
    c = lax.axis_index("ctx")
    me = lax.axis_index("head")
    flat = c * n_head + me
    total = n_ctx * n_head
    nxt = lax.rem(flat + 1, total)
    prv = lax.rem(flat + total - 1, total)
    up = lax.rem(c + 1, n_ctx)
    down = lax.rem(c + n_ctx - 1, n_ctx)

    def peer(i):
        return lax.rem(me + i, n_head)

    def at_head(h):
        return (run, c, h)

    def x_copy(q):
        at = pl.ds(pl.multiple_of(q * pieces * GROUP, GROUP), pieces * GROUP)
        return pltpu.make_async_copy(x_hbm.at[:, at], x_ref.at[:, at], x_sem.at[q])

    tail_copy = pltpu.make_async_copy(x_hbm.at[pl.ds(tokens - 16, 16)], tail_v, tail_sem)
    tail_copy.start()
    for q in range(n_head):
        x_copy(q).start()

    barrier = pltpu.get_barrier_semaphore()
    for i in range(1, n_head):
        pl.semaphore_signal(barrier, inc=1, device_id=at_head(peer(i)), device_id_type=MESH)
    for f in (nxt, prv):
        pl.semaphore_signal(
            barrier, inc=1, device_id=(run, f // n_head, lax.rem(f, n_head)), device_id_type=MESH
        )
    for z in (up, down):
        pl.semaphore_signal(barrier, inc=1, device_id=(run, z, me), device_id_type=MESH)

    part = channels // 5
    tail_copy.wait()
    tail = tail_v[...].astype(F32)
    stail = si_ref[tokens - 16:, :].astype(F32)
    eb32[...] = jnp.zeros_like(eb32)
    for i in range(5):
        eb32[3 * i:3 * i + 3, :] = tail[13:16, i * part:(i + 1) * part]
    for r in range(3):
        eb32[15:16, r * 2 * state:(r + 1) * 2 * state] = stail[13 + r:14 + r, :]
    ebs[...] = eb32[...].astype(BF16)
    cwb[me, 0:KERNEL + 1, :] = cw_ref[...]
    cwb[me, KERNEL + 1:8, :] = jnp.zeros((8 - KERNEL - 1, cw_ref.shape[1]), F32)
    own = heads // n_head
    smb[me] = jnp.zeros((8, LANES), F32)
    smb[me, 0:2, 0:own] = hr_ref[...]
    smb[me, 2:3, 0:own] = sg_ref[...]
    smb[me] = pltpu.roll(smb[me], me * own, 1)

    pl.semaphore_wait(barrier, n_head - 1 + 4)

    edge_copy = pltpu.make_async_remote_copy(
        ebs, ebr, eb_ss, eb_rs, device_id=(run, nxt // n_head, lax.rem(nxt, n_head)), device_id_type=MESH
    )
    edge_copy.start()

    def param_copies(dst, slot, k):
        return (
            pltpu.make_async_remote_copy(
                smb.at[slot], smb.at[slot], sm_ss.at[k], sm_rs.at[slot],
                device_id=at_head(dst), device_id_type=MESH),
            pltpu.make_async_remote_copy(
                cwb.at[slot], cwb.at[slot], cw_ss.at[k], cw_rs.at[slot],
                device_id=at_head(dst), device_id_type=MESH),
        )

    for i in range(1, n_head):
        for copy in param_copies(peer(i), me, i):
            copy.start()
    for i in range(1, n_head):
        param_copies(peer(i), peer(i), i)[0].wait_recv()

    small = jnp.sum(smb[...], axis=0)
    bias = small[0:1]
    rate = jnp.exp(small[1:2])
    gain = small[2:3]
    raw = jnp.concatenate(
        [sr_ref[...].astype(F32), jnp.zeros((LANES - heads, tokens), F32)], axis=0
    ).T
    step = softplus(raw + bias)
    decay = -step * rate
    rows = lax.broadcasted_iota(jnp.int32, (SPAN, SPAN), 0)
    cols = lax.broadcasted_iota(jnp.int32, (SPAN, SPAN), 1)
    lower = rows >= cols
    tri = jnp.where(lower, 1.0, 0.0).astype(F32)
    step_hl[...] = split2(step)
    ends = []
    for b in range(blocks):
        lo = b * SPAN
        cm = jnp.dot(tri, decay[lo:lo + SPAN] * LOG2E, precision=lax.Precision.HIGHEST,
                     preferred_element_type=F32)
        cum[lo:lo + SPAN, :] = cm
        cum_t[:, lo:lo + SPAN] = cm.T
        end = cm[SPAN - 1:SPAN]
        w_hl[lo:lo + SPAN, :] = split2(jnp.exp2(end - cm))
        ec_hl[lo:lo + SPAN, :] = split2(jnp.exp2(cm))
        ends.append(end)
    dec_rows = jnp.concatenate(
        [jnp.exp2(ends[0]), jnp.exp2(ends[1]), jnp.exp2(ends[0] + ends[1]), gain,
         jnp.zeros((12, LANES), F32)], axis=0)
    dec_hl[...] = split2(dec_rows)

    edge_copy.wait_recv()
    eb32[...] = jnp.where(flat == 0, 0.0, ebr[...].astype(F32))
    for i in range(5):
        edge[5:8, i * part:(i + 1) * part] = eb32[3 * i:3 * i + 3, :]
    for r in range(3):
        sedge[5 + r:6 + r, :] = eb32[15:16, r * 2 * state:(r + 1) * 2 * state]

    def conv(l, taps):
        v = taps(KERNEL) + taps(0) * xs[l, pl.ds(8 - KERNEL + 1, tokens), :]
        for k in range(1, KERNEL):
            v = v + taps(k) * xs[l, pl.ds(8 - KERNEL + 1 + k, tokens), :]
        return silu(v).astype(BF16)

    for l in range(2):
        at = pl.ds(l * LANES, LANES)
        xs[l, 0:8, :] = sedge[:, at]
        xs[l, 8:8 + tokens, :] = si_ref[:, at].astype(F32)
    b_conv = conv(0, lambda k: cs_ref[k:k + 1, 0:LANES])
    c_conv = conv(1, lambda k: cs_ref[k:k + 1, LANES:2 * LANES])
    b_t = b_conv.astype(F32).T.astype(BF16)
    bt[...] = b_t
    cc[...] = c_conv
    for b in range(blocks):
        lo = b * SPAN
        sc = dot(c_conv[lo:lo + SPAN], b_t[:, lo:lo + SPAN])
        scores[b] = jnp.where(lower, sc, 0.0)

    for i in range(1, n_head):
        param_copies(peer(i), peer(i), i)[1].wait_recv()

    def spreader(g):
        k = lax.broadcasted_iota(jnp.int32, (2 * LANES, GROUP), 0)
        l = lax.broadcasted_iota(jnp.int32, (2 * LANES, GROUP), 1)
        return jnp.where(lax.rem(k, LANES) == g * per + l // width, 1.0, 0.0).astype(BF16)

    def state_copies(dst, slot, k, j):
        return (
            pltpu.make_async_remote_copy(
                s_out.at[dst, j], slots.at[slot, j], s_ss.at[k, j], s_rs.at[slot, j],
                device_id=at_head(dst), device_id_type=MESH),
            pltpu.make_async_remote_copy(
                dx.at[dst, j], d_slots.at[slot, j], d_ss.at[k, j], d_rs.at[slot, j],
                device_id=at_head(dst), device_id_type=MESH),
        )

    def form(q, j, slot):
        g = q * pieces + j
        base = pl.multiple_of(g * GROUP, GROUP)
        jb = pl.multiple_of(j * GROUP, GROUP)
        spread = spreader(g)
        us = []
        sb = dot(step_hl[...], spread)
        wb = dot(w_hl[...], spread)
        for l in range(2):
            at = pl.ds(pl.multiple_of(base + l * LANES, LANES), LANES)
            tap_at = pl.ds(pl.multiple_of(jb + l * LANES, LANES), LANES)
            xs[2 * slot + l, 0:8, :] = edge[:, at]
            xs[2 * slot + l, 8:8 + tokens, :] = x_ref[:, at].astype(F32)
            xv = conv(2 * slot + l, lambda k: cwb[q, k:k + 1, tap_at])
            xc[:, at] = xv
            half = slice(l * LANES, (l + 1) * LANES)
            u = (xv.astype(F32) * sb[:, half]).astype(BF16)
            uv[:, at] = u
            us.append((u.astype(F32) * wb[:, half]).astype(BF16))
        uw = jnp.concatenate(us, axis=1)
        d = dot(dec_hl[...], spread)[0:8]
        dx[q, j] = d
        first = dot(bt[:, 0:SPAN], uw[0:SPAN])
        second = dot(bt[:, SPAN:2 * SPAN], uw[SPAN:2 * SPAN])
        s0[q, j] = first.astype(BF16)
        return d, (d[1:2] * first + second).astype(BF16)

    def send(i, j):
        for copy in state_copies(peer(i), me, i, j):
            copy.start()

    def form_piece(j):
        made = [form(peer(i), j, i % 2) for i in (1, 2)]
        for i in (1, 2):
            s_out[peer(i), j] = made[i - 1][1]
        for i in (1, 2):
            send(i, j)
        far = [form(peer(i), j, i % 2) for i in range(3, n_head)]
        d, mine = form(me, j, 0)
        for i in range(3, n_head):
            s_out[peer(i), j] = far[i - 3][1]
        slots[me, j] = mine
        d_slots[me, j] = d
        for i in range(3, n_head):
            send(i, j)

    lane = lax.broadcasted_iota(jnp.int32, (1, LANES), 1)

    def local(g):
        base = pl.multiple_of(g * GROUP, GROUP)
        q = g // pieces
        j = lax.rem(g, pieces)
        half = SPAN // 2
        for b in range(blocks):
            lo = b * SPAN
            turned = pltpu.roll(cum[lo:lo + SPAN, :], lax.rem(LANES - g * per, LANES), 1)
            for l in range(2):
                at = pl.ds(pl.multiple_of(base + l * LANES, LANES), LANES)
                u = uv[lo:lo + SPAN, at]
                tops, lows = [], []
                for k in range(2):
                    h = l * 2 + k
                    col = turned[:, h:h + 1]
                    row = cum_t[pl.ds(g * per + h, 1), lo:lo + SPAN]
                    top = jnp.exp2(jnp.minimum(col[0:half] - row[:, 0:half], 0.0))
                    low = jnp.exp2(jnp.minimum(col[half:SPAN] - row, 0.0))
                    top = (top * scores[b, 0:half, 0:half]).astype(BF16)
                    low = (low * scores[b, half:SPAN, :]).astype(BF16)
                    tops.append(dot(top, u[0:half]))
                    lows.append(dot(low, u))
                skip = dx[q, j, 3:4, l * LANES:(l + 1) * LANES]
                acc[lo:lo + half, at] = (
                    jnp.where(lane < width, tops[0], tops[1])
                    + skip * xc[lo:lo + half, at].astype(F32)).astype(BF16)
                acc[lo + half:lo + SPAN, at] = (
                    jnp.where(lane < width, lows[0], lows[1])
                    + skip * xc[lo + half:lo + SPAN, at].astype(F32)).astype(BF16)
        acc_copy(g).start()

    def acc_copy(g):
        at = pl.ds(pl.multiple_of(g * GROUP, GROUP), GROUP)
        return pltpu.make_async_copy(acc.at[:, at], acc_hbm.at[:, at], acc_sem.at[g])

    def chain_copy(j):
        return pltpu.make_async_remote_copy(
            ch_out.at[j], ch_in.at[j], ch_ss.at[j], ch_rs.at[j],
            device_id=(run, up, me), device_id_type=MESH)

    def back_copy(dst, slot, k, j):
        return pltpu.make_async_remote_copy(
            p_out.at[dst, j], inc.at[slot, j], p_ss.at[k, j], p_rs.at[slot, j],
            device_id=at_head(dst), device_id_type=MESH)

    def own_copy(j):
        return pltpu.make_async_copy(p_out.at[me, j], inc.at[me, j], own_sem.at[j])

    def chain_piece(j):
        for i in range(1, n_head):
            for copy in state_copies(peer(i), peer(i), i, j):
                copy.wait_recv()
        q_sum = slots[0, j].astype(F32)
        r = d_slots[0, j, 2:3]
        for e in range(1, n_head):
            d = d_slots[e, j, 2:3]
            q_sum = d * q_sum + slots[e, j].astype(F32)
            r = d * r

        @pl.when(c > 0)
        def _():
            chain_copy(j).wait_recv()

        @pl.when(c == 0)
        def _():
            ch_in[j] = jnp.zeros((state, GROUP), BF16)

        arriving = ch_in[j].astype(F32)
        ch_out[j] = (r * arriving + q_sum).astype(BF16)

        @pl.when(c < n_ctx - 1)
        def _():
            chain_copy(j).start()

        prefix = arriving
        p_out[0, j] = prefix.astype(BF16)
        for e in range(1, n_head):
            prefix = d_slots[e - 1, j, 2:3] * prefix + slots[e - 1, j].astype(F32)
            p_out[e, j] = prefix.astype(BF16)
        for i in range(1, n_head):
            back_copy(peer(i), me, i, j).start()
        own_copy(j).start()

    units = n_head * pieces
    every = 3
    turns = pieces + (units - 1) // every + 1
    lag = jnp.minimum(c, turns - 1 - pieces)

    def chain_turn(turn):
        p = turn - 1 - lag

        @pl.when(jnp.logical_and(p >= 0, p < pieces))
        def _():
            chain_piece(p)

    for q in range(n_head):
        x_copy(q).wait()

    def form_turn(j, carry):
        form_piece(j)
        chain_turn(j)
        return carry

    lax.fori_loop(0, pieces, form_turn, 0)
    s0_copy = pltpu.make_async_copy(s0, s0_hbm, s0_sem)
    s0_copy.start()

    def local_turn(u, carry):
        local(u)

        @pl.when(lax.rem(u, every) == 0)
        def _():
            chain_turn(pieces + u // every)
        return carry

    lax.fori_loop(0, units, local_turn, 0)

    edge_copy.wait_send()
    for i in range(1, n_head):
        for copy in param_copies(peer(i), me, i):
            copy.wait_send()

    def drain(j, carry):
        for i in range(1, n_head):
            for copy in state_copies(peer(i), me, i, j):
                copy.wait_send()
            back_copy(peer(i), me, i, j).wait_send()

            back_copy(peer(i), peer(i), i, j).wait_recv()
        own_copy(j).wait()

        @pl.when(c < n_ctx - 1)
        def _():
            chain_copy(j).wait_send()
        return carry

    lax.fori_loop(0, pieces, drain, 0)
    s0_copy.wait()

    def drain_acc(g, carry):
        acc_copy(g).wait()
        return carry

    lax.fori_loop(0, units, drain_acc, 0)


def finish(width, acc_ref, inc_ref, s0_ref, dx_ref, ec_ref, cc_ref, out_ref):
    q = pl.program_id(0)
    pieces = inc_ref.shape[1]
    per = GROUP // width
    for j in range(pieces):
        k = lax.broadcasted_iota(jnp.int32, (2 * LANES, GROUP), 0)
        l = lax.broadcasted_iota(jnp.int32, (2 * LANES, GROUP), 1)
        place = (q * pieces + j) * per + l // width
        spread = jnp.where(lax.rem(k, LANES) == place, 1.0, 0.0).astype(BF16)
        entering = inc_ref[0, j]
        middle = (dx_ref[0, j, 0:1] * entering.astype(F32) + s0_ref[0, j].astype(F32)).astype(BF16)
        at = slice(j * GROUP, (j + 1) * GROUP)
        for b, held in enumerate((entering, middle)):
            rows = slice(b * SPAN, (b + 1) * SPAN)
            carried = dot(ec_ref[rows, :], spread) * dot(cc_ref[rows, :], held)
            out_ref[rows, at] = (acc_ref[rows, at].astype(F32) + carried).astype(BF16)


def per_device(n_ctx, n_head, inner_tokens, state_inputs, step_raw, conv_inner, conv_state, head_rates, skip_gain):
    tokens, channels = inner_tokens.shape
    heads = step_raw.shape[1]
    width = channels // heads
    state = state_inputs.shape[1] // 2
    pieces = channels // n_head // GROUP
    part = channels // n_head
    vm = pltpu.VMEM
    dma = pltpu.SemaphoreType.DMA
    grid4 = (n_head, pieces, state, GROUP)
    small4 = (n_head, pieces, 8, GROUP)
    scratch = [
        vm((tokens, channels), BF16), vm((16, channels), BF16),
        vm((n_head, 8, part), F32), vm((n_head, 8, LANES), F32),
        vm((16, channels // 5), F32), vm((16, channels // 5), BF16), vm((16, channels // 5), BF16),
        vm((8, channels), F32), vm((8, 2 * state), F32), vm((4, tokens + 8, LANES), F32),
        vm((tokens, LANES), F32), vm((LANES, tokens), F32),
        vm((tokens, 2 * LANES), BF16), vm((tokens, 2 * LANES), BF16),
        vm((16, 2 * LANES), BF16),
        vm((tokens // SPAN, SPAN, SPAN), F32), vm((state, tokens), BF16),
        vm((tokens, channels), BF16), vm((tokens, channels), BF16), vm((tokens, channels), BF16),
        vm(grid4, BF16), vm(grid4, BF16), vm(grid4, BF16), vm(small4, F32),
        vm((pieces, state, GROUP), BF16), vm((pieces, state, GROUP), BF16),
        vm(grid4, BF16),
        dma((n_head,)), dma((n_head,)), dma((n_head,)), dma((n_head,)),
        dma, dma,
        dma((n_head, pieces)), dma((n_head, pieces)), dma((n_head, pieces)), dma((n_head, pieces)),
        dma((pieces,)), dma((pieces,)),
        dma((n_head, pieces)), dma((n_head, pieces)),
        dma((n_head,)), dma, dma((n_head * pieces,)), dma, dma((pieces,)),
    ]
    in_vmem = pl.BlockSpec(memory_space=pltpu.VMEM)
    anywhere = pl.BlockSpec(memory_space=pl.ANY)
    shape = jax.ShapeDtypeStruct
    parts = pl.pallas_call(
        functools.partial(kernel, n_ctx, n_head, heads, width, pieces),
        out_shape=(
            shape((tokens, channels), BF16), shape(grid4, BF16), shape(grid4, BF16),
            shape(small4, F32), shape((tokens, 2 * LANES), BF16), shape((tokens, state), BF16),
        ),
        in_specs=[anywhere] + [in_vmem] * 6,
        out_specs=(anywhere, anywhere, anywhere, in_vmem, in_vmem, in_vmem),
        scratch_shapes=scratch,
        compiler_params=pltpu.CompilerParams(
            collective_id=0, has_side_effects=True, vmem_limit_bytes=56 * 1024 * 1024
        ),
        name="ssd_layer",
    )(inner_tokens, state_inputs, step_raw.T, conv_inner, conv_state, head_rates, skip_gain[None])
    column = pl.BlockSpec((tokens, part), lambda q: (0, q))
    states = pl.BlockSpec((1, pieces, state, GROUP), lambda q: (q, 0, 0, 0))
    return pl.pallas_call(
        functools.partial(finish, width),
        grid=(n_head,),
        out_shape=shape((tokens, channels), BF16),
        in_specs=[
            column, states, states,
            pl.BlockSpec((1, pieces, 8, GROUP), lambda q: (q, 0, 0, 0)),
            pl.BlockSpec((tokens, 2 * LANES), lambda q: (0, 0)),
            pl.BlockSpec((tokens, state), lambda q: (0, 0)),
        ],
        out_specs=column,
        compiler_params=pltpu.CompilerParams(vmem_limit_bytes=56 * 1024 * 1024),
        name="carried_terms",
    )(*parts)


def solution(mesh):
    return jax.shard_map(
        functools.partial(per_device, mesh.shape["ctx"], mesh.shape["head"]),
        mesh=mesh,
        in_specs=(
            P(("run", "ctx", "head"), None),
            P(("run", "ctx", "head"), None),
            P(("run", "ctx", "head"), None),
            P(None, "head"),
            P(),
            P("run", "head"),
            P("head"),
        ),
        out_specs=P(("run", "ctx", "head"), None),
        check_vma=False,
    )
```

```python
import functools

import jax
import jax.numpy as jnp
from jax import lax
from jax.experimental import pallas as pl
from jax.experimental.pallas import tpu as pltpu
from jax.sharding import PartitionSpec as P

KERNEL = 4
SPAN = 256
GROUP = 256
LANES = 128
LOG2E = 1.4426950408889634
F32 = jnp.float32
BF16 = jnp.bfloat16
MESH = pl.DeviceIdType.MESH


def dot(a, b):
    return jnp.dot(a, b, preferred_element_type=F32)


def split2(v):
    hi = v.astype(BF16)
    lo = (v - hi.astype(F32)).astype(BF16)
    return jnp.concatenate([hi, lo], axis=1)


def silu(v):
    return v * (0.5 + 0.5 * jnp.tanh(0.5 * v))


def softplus(v):
    return jnp.maximum(v, 0.0) + jnp.log(1.0 + jnp.exp(-jnp.abs(v)))


def spread_matrix(first, width):
    k = lax.broadcasted_iota(jnp.int32, (LANES, GROUP), 0)
    l = lax.broadcasted_iota(jnp.int32, (LANES, GROUP), 1)
    place = k - jnp.right_shift(l, width.bit_length() - 1)
    once = jnp.where(place == first, 1.0, 0.0).astype(BF16)
    return jnp.concatenate([once, once], axis=0)


def kernel(
    n_ctx, n_head, heads, width, pieces,
    x_hbm, si_ref, sr_ref, cw_ref, cs_ref, hr_ref, sg_ref,
    acc_hbm, inc, s0_hbm, dx, ec_hl, cc,
    x_ref, tail_v, cwb, smb, eb32, ebs, ebr, edge, sedge, xs,
    cum, cum_t, step_hl, w_hl, dec_hl, scores, bt,
    xc, uv, acc, s0, s_out, slots, d_slots, ch_in, ch_out, p_out,
    cw_ss, cw_rs, sm_ss, sm_rs, eb_ss, eb_rs, s_ss, s_rs, d_ss, d_rs, ch_ss, ch_rs, p_ss, p_rs,
    x_sem, tail_sem, acc_sem, s0_sem, own_sem,
):
    tokens, channels = x_ref.shape
    blocks = tokens // SPAN
    per = GROUP // width
    state = cc.shape[1]
    run = lax.axis_index("run")
    c = lax.axis_index("ctx")
    me = lax.axis_index("head")
    flat = c * n_head + me
    total = n_ctx * n_head
    nxt = lax.rem(flat + 1, total)
    prv = lax.rem(flat + total - 1, total)
    up = lax.rem(c + 1, n_ctx)
    down = lax.rem(c + n_ctx - 1, n_ctx)

    def peer(i):
        return lax.rem(me + i, n_head)

    def at_head(h):
        return (run, c, h)

    def x_copy(q):
        at = pl.ds(pl.multiple_of(q * pieces * GROUP, GROUP), pieces * GROUP)
        return pltpu.make_async_copy(x_hbm.at[:, at], x_ref.at[:, at], x_sem.at[q])

    tail_copy = pltpu.make_async_copy(x_hbm.at[pl.ds(tokens - 16, 16)], tail_v, tail_sem)
    tail_copy.start()
    for q in range(n_head):
        x_copy(q).start()

    barrier = pltpu.get_barrier_semaphore()
    for i in range(1, n_head):
        pl.semaphore_signal(barrier, inc=1, device_id=at_head(peer(i)), device_id_type=MESH)
    for f in (nxt, prv):
        pl.semaphore_signal(
            barrier, inc=1, device_id=(run, f // n_head, lax.rem(f, n_head)), device_id_type=MESH
        )
    for z in (up, down):
        pl.semaphore_signal(barrier, inc=1, device_id=(run, z, me), device_id_type=MESH)

    part = channels // 5
    tail_copy.wait()
    tail = tail_v[...].astype(F32)
    stail = si_ref[tokens - 16:, :].astype(F32)
    eb32[...] = jnp.zeros_like(eb32)
    for i in range(5):
        eb32[3 * i:3 * i + 3, :] = tail[13:16, i * part:(i + 1) * part]
    for r in range(3):
        eb32[15:16, r * 2 * state:(r + 1) * 2 * state] = stail[13 + r:14 + r, :]
    ebs[...] = eb32[...].astype(BF16)
    cwb[me, 0:KERNEL + 1, :] = cw_ref[...]
    cwb[me, KERNEL + 1:8, :] = jnp.zeros((8 - KERNEL - 1, cw_ref.shape[1]), F32)
    own = heads // n_head
    smb[me] = jnp.zeros((8, LANES), F32)
    smb[me, 0:2, 0:own] = hr_ref[...]
    smb[me, 2:3, 0:own] = sg_ref[...]
    smb[me] = pltpu.roll(smb[me], me * own, 1)

    pl.semaphore_wait(barrier, n_head - 1 + 4)

    edge_copy = pltpu.make_async_remote_copy(
        ebs, ebr, eb_ss, eb_rs, device_id=(run, nxt // n_head, lax.rem(nxt, n_head)), device_id_type=MESH
    )
    edge_copy.start()

    def param_copies(dst, slot, k):
        return (
            pltpu.make_async_remote_copy(
                smb.at[slot], smb.at[slot], sm_ss.at[k], sm_rs.at[slot],
                device_id=at_head(dst), device_id_type=MESH),
            pltpu.make_async_remote_copy(
                cwb.at[slot], cwb.at[slot], cw_ss.at[k], cw_rs.at[slot],
                device_id=at_head(dst), device_id_type=MESH),
        )

    for i in range(1, n_head):
        for copy in param_copies(peer(i), me, i):
            copy.start()
    for i in range(1, n_head):
        param_copies(peer(i), peer(i), i)[0].wait_recv()

    small = jnp.sum(smb[...], axis=0)
    bias = small[0:1]
    rate = jnp.exp(small[1:2])
    gain = small[2:3]
    raw = jnp.concatenate(
        [sr_ref[...].astype(F32), jnp.zeros((LANES - heads, tokens), F32)], axis=0
    ).T
    step = softplus(raw + bias)
    decay = -step * rate
    rows = lax.broadcasted_iota(jnp.int32, (SPAN, SPAN), 0)
    cols = lax.broadcasted_iota(jnp.int32, (SPAN, SPAN), 1)
    lower = rows >= cols
    tri = jnp.where(lower, 1.0, 0.0).astype(F32)
    step_hl[...] = split2(step)
    ends = []
    for b in range(blocks):
        lo = b * SPAN
        cm = jnp.dot(tri, decay[lo:lo + SPAN] * LOG2E, precision=lax.Precision.HIGHEST,
                     preferred_element_type=F32)
        cum[lo:lo + SPAN, :] = cm
        cum_t[:, lo:lo + SPAN] = cm.T
        end = cm[SPAN - 1:SPAN]
        w_hl[lo:lo + SPAN, :] = split2(jnp.exp2(end - cm))
        ec_hl[lo:lo + SPAN, :] = split2(jnp.exp2(cm))
        ends.append(end)
    dec_rows = jnp.concatenate(
        [jnp.exp2(ends[0]), jnp.exp2(ends[1]), jnp.exp2(ends[0] + ends[1]), gain,
         jnp.zeros((12, LANES), F32)], axis=0)
    dec_hl[...] = split2(dec_rows)

    edge_copy.wait_recv()
    eb32[...] = jnp.where(flat == 0, 0.0, ebr[...].astype(F32))
    for i in range(5):
        edge[5:8, i * part:(i + 1) * part] = eb32[3 * i:3 * i + 3, :]
    for r in range(3):
        sedge[5 + r:6 + r, :] = eb32[15:16, r * 2 * state:(r + 1) * 2 * state]

    def conv(l, taps):
        v = taps(KERNEL) + taps(0) * xs[l, pl.ds(8 - KERNEL + 1, tokens), :]
        for k in range(1, KERNEL):
            v = v + taps(k) * xs[l, pl.ds(8 - KERNEL + 1 + k, tokens), :]
        return silu(v).astype(BF16)

    for l in range(2):
        at = pl.ds(l * LANES, LANES)
        xs[l, 0:8, :] = sedge[:, at]
        xs[l, 8:8 + tokens, :] = si_ref[:, at].astype(F32)
    b_conv = conv(0, lambda k: cs_ref[k:k + 1, 0:LANES])
    c_conv = conv(1, lambda k: cs_ref[k:k + 1, LANES:2 * LANES])
    b_t = b_conv.astype(F32).T.astype(BF16)
    bt[...] = b_t
    cc[...] = c_conv
    for b in range(blocks):
        lo = b * SPAN
        sc = dot(c_conv[lo:lo + SPAN], b_t[:, lo:lo + SPAN])
        scores[b] = jnp.where(lower, sc, 0.0)

    for i in range(1, n_head):
        param_copies(peer(i), peer(i), i)[1].wait_recv()

    def spreader(g):
        return spread_matrix(g * per, width)

    def state_copies(dst, slot, k, j):
        return (
            pltpu.make_async_remote_copy(
                s_out.at[dst, j], slots.at[slot, j], s_ss.at[k, j], s_rs.at[slot, j],
                device_id=at_head(dst), device_id_type=MESH),
            pltpu.make_async_remote_copy(
                dx.at[dst, j], d_slots.at[slot, j], d_ss.at[k, j], d_rs.at[slot, j],
                device_id=at_head(dst), device_id_type=MESH),
        )

    def form(q, j, slot):
        g = q * pieces + j
        base = pl.multiple_of(g * GROUP, GROUP)
        jb = pl.multiple_of(j * GROUP, GROUP)
        spread = spreader(g)
        us = []
        sb = dot(step_hl[...], spread)
        wb = dot(w_hl[...], spread)
        for l in range(2):
            at = pl.ds(pl.multiple_of(base + l * LANES, LANES), LANES)
            tap_at = pl.ds(pl.multiple_of(jb + l * LANES, LANES), LANES)
            xs[2 * slot + l, 0:8, :] = edge[:, at]
            xs[2 * slot + l, 8:8 + tokens, :] = x_ref[:, at].astype(F32)
            xv = conv(2 * slot + l, lambda k: cwb[q, k:k + 1, tap_at])
            xc[:, at] = xv
            half = slice(l * LANES, (l + 1) * LANES)
            u = (xv.astype(F32) * sb[:, half]).astype(BF16)
            uv[:, at] = u
            us.append((u.astype(F32) * wb[:, half]).astype(BF16))
        uw = jnp.concatenate(us, axis=1)
        d = dot(dec_hl[...], spread)[0:8]
        dx[q, j] = d
        first = dot(bt[:, 0:SPAN], uw[0:SPAN])
        second = dot(bt[:, SPAN:2 * SPAN], uw[SPAN:2 * SPAN])
        s0[q, j] = first.astype(BF16)
        return d, (d[1:2] * first + second).astype(BF16)

    def send(i, j):
        for copy in state_copies(peer(i), me, i, j):
            copy.start()

    def form_piece(j):
        made = [form(peer(i), j, i % 2) for i in (1, 2)]
        for i in (1, 2):
            s_out[peer(i), j] = made[i - 1][1]
        for i in (1, 2):
            send(i, j)
        far = [form(peer(i), j, i % 2) for i in range(3, n_head)]
        d, mine = form(me, j, 0)
        for i in range(3, n_head):
            s_out[peer(i), j] = far[i - 3][1]
        slots[me, j] = mine
        d_slots[me, j] = d
        for i in range(3, n_head):
            send(i, j)

    lane = lax.broadcasted_iota(jnp.int32, (1, LANES), 1)

    def local(g):
        base = pl.multiple_of(g * GROUP, GROUP)
        q = g // pieces
        j = lax.rem(g, pieces)
        half = SPAN // 2
        for b in range(blocks):
            lo = b * SPAN
            turned = pltpu.roll(cum[lo:lo + SPAN, :], lax.rem(LANES - g * per, LANES), 1)
            for l in range(2):
                at = pl.ds(pl.multiple_of(base + l * LANES, LANES), LANES)
                u = uv[lo:lo + SPAN, at]
                mixing = []
                for k in range(2):
                    h = l * 2 + k
                    col = turned[:, h:h + 1]
                    row = cum_t[pl.ds(g * per + h, 1), lo:lo + SPAN]
                    top = jnp.exp2(jnp.minimum(col[0:half] - row[:, 0:half], 0.0))
                    low = jnp.exp2(jnp.minimum(col[half:SPAN] - row, 0.0))
                    top = (top * scores[b, 0:half, 0:half]).astype(BF16)
                    low = (low * scores[b, half:SPAN, :]).astype(BF16)
                    mixing += [jnp.concatenate([top, jnp.zeros_like(top)], axis=1), low]
                made = dot(jnp.concatenate(mixing, axis=0), u)
                local_terms = jnp.where(lane < width, made[0:SPAN], made[SPAN:2 * SPAN])
                skip = dx[q, j, 3:4, l * LANES:(l + 1) * LANES]
                acc[lo:lo + SPAN, at] = (
                    local_terms + skip * xc[lo:lo + SPAN, at].astype(F32)).astype(BF16)
        acc_copy(g).start()

    def acc_copy(g):
        at = pl.ds(pl.multiple_of(g * GROUP, GROUP), GROUP)
        return pltpu.make_async_copy(acc.at[:, at], acc_hbm.at[:, at], acc_sem.at[g])

    def chain_copy(j):
        return pltpu.make_async_remote_copy(
            ch_out.at[j], ch_in.at[j], ch_ss.at[j], ch_rs.at[j],
            device_id=(run, up, me), device_id_type=MESH)

    def back_copy(dst, slot, k, j):
        return pltpu.make_async_remote_copy(
            p_out.at[dst, j], inc.at[slot, j], p_ss.at[k, j], p_rs.at[slot, j],
            device_id=at_head(dst), device_id_type=MESH)

    def own_copy(j):
        return pltpu.make_async_copy(p_out.at[me, j], inc.at[me, j], own_sem.at[j])

    def chain_piece(j):
        for i in range(1, n_head):
            for copy in state_copies(peer(i), peer(i), i, j):
                copy.wait_recv()
        q_sum = slots[0, j].astype(F32)
        r = d_slots[0, j, 2:3]
        for e in range(1, n_head):
            d = d_slots[e, j, 2:3]
            q_sum = d * q_sum + slots[e, j].astype(F32)
            r = d * r

        @pl.when(c > 0)
        def _():
            chain_copy(j).wait_recv()

        @pl.when(c == 0)
        def _():
            ch_in[j] = jnp.zeros((state, GROUP), BF16)

        arriving = ch_in[j].astype(F32)
        ch_out[j] = (r * arriving + q_sum).astype(BF16)

        @pl.when(c < n_ctx - 1)
        def _():
            chain_copy(j).start()

        prefix = arriving
        p_out[0, j] = prefix.astype(BF16)
        for e in range(1, n_head):
            prefix = d_slots[e - 1, j, 2:3] * prefix + slots[e - 1, j].astype(F32)
            p_out[e, j] = prefix.astype(BF16)
        for i in range(1, n_head):
            back_copy(peer(i), me, i, j).start()
        own_copy(j).start()

    units = n_head * pieces
    every = 3
    turns = pieces + (units - 1) // every + 1
    lag = jnp.minimum(c, turns - 1 - pieces)

    def chain_turn(turn):
        p = turn - 1 - lag

        @pl.when(jnp.logical_and(p >= 0, p < pieces))
        def _():
            chain_piece(p)

    for q in range(n_head):
        x_copy(q).wait()

    def form_turn(j, carry):
        form_piece(j)
        chain_turn(j)
        return carry

    lax.fori_loop(0, pieces, form_turn, 0)
    s0_copy = pltpu.make_async_copy(s0, s0_hbm, s0_sem)
    s0_copy.start()

    def local_turn(u, carry):
        local(u)

        @pl.when(lax.rem(u, every) == 0)
        def _():
            chain_turn(pieces + u // every)
        return carry

    lax.fori_loop(0, units, local_turn, 0)

    edge_copy.wait_send()
    for i in range(1, n_head):
        for copy in param_copies(peer(i), me, i):
            copy.wait_send()

    def drain(j, carry):
        for i in range(1, n_head):
            for copy in state_copies(peer(i), me, i, j):
                copy.wait_send()
            back_copy(peer(i), me, i, j).wait_send()

            back_copy(peer(i), peer(i), i, j).wait_recv()
        own_copy(j).wait()

        @pl.when(c < n_ctx - 1)
        def _():
            chain_copy(j).wait_send()
        return carry

    lax.fori_loop(0, pieces, drain, 0)
    s0_copy.wait()

    def drain_acc(g, carry):
        acc_copy(g).wait()
        return carry

    lax.fori_loop(0, units, drain_acc, 0)


def finish(width, acc_ref, inc_ref, s0_ref, dx_ref, ec_ref, cc_ref, out_ref):
    q = pl.program_id(0)
    pieces = inc_ref.shape[1]
    per = GROUP // width
    for j in range(pieces):
        spread = spread_matrix((q * pieces + j) * per, width)
        entering = inc_ref[0, j]
        middle = (dx_ref[0, j, 0:1] * entering.astype(F32) + s0_ref[0, j].astype(F32)).astype(BF16)
        at = slice(j * GROUP, (j + 1) * GROUP)
        for b, held in enumerate((entering, middle)):
            rows = slice(b * SPAN, (b + 1) * SPAN)
            carried = dot(ec_ref[rows, :], spread) * dot(cc_ref[rows, :], held)
            out_ref[rows, at] = (acc_ref[rows, at].astype(F32) + carried).astype(BF16)


def per_device(n_ctx, n_head, inner_tokens, state_inputs, step_raw, conv_inner, conv_state, head_rates, skip_gain):
    tokens, channels = inner_tokens.shape
    heads = step_raw.shape[1]
    width = channels // heads
    state = state_inputs.shape[1] // 2
    pieces = channels // n_head // GROUP
    part = channels // n_head
    vm = pltpu.VMEM
    dma = pltpu.SemaphoreType.DMA
    grid4 = (n_head, pieces, state, GROUP)
    small4 = (n_head, pieces, 8, GROUP)
    scratch = [
        vm((tokens, channels), BF16), vm((16, channels), BF16),
        vm((n_head, 8, part), F32), vm((n_head, 8, LANES), F32),
        vm((16, channels // 5), F32), vm((16, channels // 5), BF16), vm((16, channels // 5), BF16),
        vm((8, channels), F32), vm((8, 2 * state), F32), vm((4, tokens + 8, LANES), F32),
        vm((tokens, LANES), F32), vm((LANES, tokens), F32),
        vm((tokens, 2 * LANES), BF16), vm((tokens, 2 * LANES), BF16),
        vm((16, 2 * LANES), BF16),
        vm((tokens // SPAN, SPAN, SPAN), F32), vm((state, tokens), BF16),
        vm((tokens, channels), BF16), vm((tokens, channels), BF16), vm((tokens, channels), BF16),
        vm(grid4, BF16), vm(grid4, BF16), vm(grid4, BF16), vm(small4, F32),
        vm((pieces, state, GROUP), BF16), vm((pieces, state, GROUP), BF16),
        vm(grid4, BF16),
        dma((n_head,)), dma((n_head,)), dma((n_head,)), dma((n_head,)),
        dma, dma,
        dma((n_head, pieces)), dma((n_head, pieces)), dma((n_head, pieces)), dma((n_head, pieces)),
        dma((pieces,)), dma((pieces,)),
        dma((n_head, pieces)), dma((n_head, pieces)),
        dma((n_head,)), dma, dma((n_head * pieces,)), dma, dma((pieces,)),
    ]
    in_vmem = pl.BlockSpec(memory_space=pltpu.VMEM)
    anywhere = pl.BlockSpec(memory_space=pl.ANY)
    shape = jax.ShapeDtypeStruct
    parts = pl.pallas_call(
        functools.partial(kernel, n_ctx, n_head, heads, width, pieces),
        out_shape=(
            shape((tokens, channels), BF16), shape(grid4, BF16), shape(grid4, BF16),
            shape(small4, F32), shape((tokens, 2 * LANES), BF16), shape((tokens, state), BF16),
        ),
        in_specs=[anywhere] + [in_vmem] * 6,
        out_specs=(anywhere, anywhere, anywhere, in_vmem, in_vmem, in_vmem),
        scratch_shapes=scratch,
        compiler_params=pltpu.CompilerParams(
            collective_id=0, has_side_effects=True, vmem_limit_bytes=56 * 1024 * 1024
        ),
        name="ssd_layer",
    )(inner_tokens, state_inputs, step_raw.T, conv_inner, conv_state, head_rates, skip_gain[None])
    column = pl.BlockSpec((tokens, part), lambda q: (0, q))
    states = pl.BlockSpec((1, pieces, state, GROUP), lambda q: (q, 0, 0, 0))
    return pl.pallas_call(
        functools.partial(finish, width),
        grid=(n_head,),
        out_shape=shape((tokens, channels), BF16),
        in_specs=[
            column, states, states,
            pl.BlockSpec((1, pieces, 8, GROUP), lambda q: (q, 0, 0, 0)),
            pl.BlockSpec((tokens, 2 * LANES), lambda q: (0, 0)),
            pl.BlockSpec((tokens, state), lambda q: (0, 0)),
        ],
        out_specs=column,
        compiler_params=pltpu.CompilerParams(vmem_limit_bytes=56 * 1024 * 1024),
        name="carried_terms",
    )(*parts)


def solution(mesh):
    return jax.shard_map(
        functools.partial(per_device, mesh.shape["ctx"], mesh.shape["head"]),
        mesh=mesh,
        in_specs=(
            P(("run", "ctx", "head"), None),
            P(("run", "ctx", "head"), None),
            P(("run", "ctx", "head"), None),
            P(None, "head"),
            P(),
            P("run", "head"),
            P("head"),
        ),
        out_specs=P(("run", "ctx", "head"), None),
        check_vma=False,
    )
```

```python
import functools

import jax
import jax.numpy as jnp
from jax import lax
from jax.experimental import pallas as pl
from jax.experimental.pallas import tpu as pltpu
from jax.sharding import PartitionSpec as P

KERNEL = 4
SPAN = 256
GROUP = 256
LANES = 128
CHUNK = 64
LOG2E = 1.4426950408889634
F32 = jnp.float32
BF16 = jnp.bfloat16
MESH = pl.DeviceIdType.MESH


def dot(a, b):
    return jnp.dot(a, b, preferred_element_type=F32)


def split2(v):
    hi = v.astype(BF16)
    lo = (v - hi.astype(F32)).astype(BF16)
    return jnp.concatenate([hi, lo], axis=1)


def silu(v):
    return v * (0.5 + 0.5 * jnp.tanh(0.5 * v))


def softplus(v):
    return jnp.maximum(v, 0.0) + jnp.log(1.0 + jnp.exp(-jnp.abs(v)))


def spread_matrix(first, width):
    k = lax.broadcasted_iota(jnp.int32, (LANES, GROUP), 0)
    l = lax.broadcasted_iota(jnp.int32, (LANES, GROUP), 1)
    place = k - jnp.right_shift(l, width.bit_length() - 1)
    once = jnp.where(place == first, 1.0, 0.0).astype(BF16)
    return jnp.concatenate([once, once], axis=0)


def kernel(
    n_ctx, n_head, heads, width, pieces,
    x_hbm, si_ref, sr_ref, cw_ref, cs_ref, hr_ref, sg_ref,
    acc_hbm, inc, s0_hbm, dx, ec_hl, cc,
    x_ref, tail_v, cwb, smb, eb32, ebs, ebr, edge, sedge, xs,
    cum, cum_t, step_hl, w_hl, dec_hl, scores, bt,
    xc, uv, uw, mix, acc, s0, s_out, slots, d_slots, ch_in, ch_out, p_out,
    cw_ss, cw_rs, sm_ss, sm_rs, eb_ss, eb_rs, s_ss, s_rs, d_ss, d_rs, ch_ss, ch_rs, p_ss, p_rs,
    x_sem, tail_sem, acc_sem, s0_sem, own_sem,
):
    tokens, channels = x_ref.shape
    blocks = tokens // SPAN
    per = GROUP // width
    state = cc.shape[1]
    run = lax.axis_index("run")
    c = lax.axis_index("ctx")
    me = lax.axis_index("head")
    flat = c * n_head + me
    total = n_ctx * n_head
    nxt = lax.rem(flat + 1, total)
    prv = lax.rem(flat + total - 1, total)
    up = lax.rem(c + 1, n_ctx)
    down = lax.rem(c + n_ctx - 1, n_ctx)

    def peer(i):
        return lax.rem(me + i, n_head)

    def at_head(h):
        return (run, c, h)

    def x_copy(q):
        at = pl.ds(pl.multiple_of(q * pieces * GROUP, GROUP), pieces * GROUP)
        return pltpu.make_async_copy(x_hbm.at[:, at], x_ref.at[:, at], x_sem.at[q])

    tail_copy = pltpu.make_async_copy(x_hbm.at[pl.ds(tokens - 16, 16)], tail_v, tail_sem)
    tail_copy.start()
    for q in range(n_head):
        x_copy(q).start()

    barrier = pltpu.get_barrier_semaphore()
    for i in range(1, n_head):
        pl.semaphore_signal(barrier, inc=1, device_id=at_head(peer(i)), device_id_type=MESH)
    for f in (nxt, prv):
        pl.semaphore_signal(
            barrier, inc=1, device_id=(run, f // n_head, lax.rem(f, n_head)), device_id_type=MESH
        )
    for z in (up, down):
        pl.semaphore_signal(barrier, inc=1, device_id=(run, z, me), device_id_type=MESH)

    part = channels // 5
    tail_copy.wait()
    tail = tail_v[...].astype(F32)
    stail = si_ref[tokens - 16:, :].astype(F32)
    eb32[...] = jnp.zeros_like(eb32)
    for i in range(5):
        eb32[3 * i:3 * i + 3, :] = tail[13:16, i * part:(i + 1) * part]
    for r in range(3):
        eb32[15:16, r * 2 * state:(r + 1) * 2 * state] = stail[13 + r:14 + r, :]
    ebs[...] = eb32[...].astype(BF16)
    cwb[me, 0:KERNEL + 1, :] = cw_ref[...]
    cwb[me, KERNEL + 1:8, :] = jnp.zeros((8 - KERNEL - 1, cw_ref.shape[1]), F32)
    own = heads // n_head
    smb[me] = jnp.zeros((8, LANES), F32)
    smb[me, 0:2, 0:own] = hr_ref[...]
    smb[me, 2:3, 0:own] = sg_ref[...]
    smb[me] = pltpu.roll(smb[me], me * own, 1)

    pl.semaphore_wait(barrier, n_head - 1 + 4)

    edge_copy = pltpu.make_async_remote_copy(
        ebs, ebr, eb_ss, eb_rs, device_id=(run, nxt // n_head, lax.rem(nxt, n_head)), device_id_type=MESH
    )
    edge_copy.start()

    def param_copies(dst, slot, k):
        return (
            pltpu.make_async_remote_copy(
                smb.at[slot], smb.at[slot], sm_ss.at[k], sm_rs.at[slot],
                device_id=at_head(dst), device_id_type=MESH),
            pltpu.make_async_remote_copy(
                cwb.at[slot], cwb.at[slot], cw_ss.at[k], cw_rs.at[slot],
                device_id=at_head(dst), device_id_type=MESH),
        )

    for i in range(1, n_head):
        for copy in param_copies(peer(i), me, i):
            copy.start()
    for i in range(1, n_head):
        param_copies(peer(i), peer(i), i)[0].wait_recv()

    small = jnp.sum(smb[...], axis=0)
    bias = small[0:1]
    rate = jnp.exp(small[1:2])
    gain = small[2:3]
    raw = jnp.concatenate(
        [sr_ref[...].astype(F32), jnp.zeros((LANES - heads, tokens), F32)], axis=0
    ).T
    step = softplus(raw + bias)
    decay = -step * rate
    rows = lax.broadcasted_iota(jnp.int32, (SPAN, SPAN), 0)
    cols = lax.broadcasted_iota(jnp.int32, (SPAN, SPAN), 1)
    lower = rows >= cols
    tri = jnp.where(lower, 1.0, 0.0).astype(F32)
    step_hl[...] = split2(step)
    ends = []
    for b in range(blocks):
        lo = b * SPAN
        cm = jnp.dot(tri, decay[lo:lo + SPAN] * LOG2E, precision=lax.Precision.HIGHEST,
                     preferred_element_type=F32)
        cum[lo:lo + SPAN, :] = cm
        cum_t[:, lo:lo + SPAN] = cm.T
        end = cm[SPAN - 1:SPAN]
        w_hl[lo:lo + SPAN, :] = split2(jnp.exp2(end - cm))
        ec_hl[lo:lo + SPAN, :] = split2(jnp.exp2(cm))
        ends.append(end)
    dec_rows = jnp.concatenate(
        [jnp.exp2(ends[0]), jnp.exp2(ends[1]), jnp.exp2(ends[0] + ends[1]), gain,
         jnp.zeros((12, LANES), F32)], axis=0)
    dec_hl[...] = split2(dec_rows)

    edge_copy.wait_recv()
    eb32[...] = jnp.where(flat == 0, 0.0, ebr[...].astype(F32))
    for i in range(5):
        edge[5:8, i * part:(i + 1) * part] = eb32[3 * i:3 * i + 3, :]
    for r in range(3):
        sedge[5 + r:6 + r, :] = eb32[15:16, r * 2 * state:(r + 1) * 2 * state]

    def conv(l, taps, start, count):
        v = taps(KERNEL) + taps(0) * xs[l, pl.ds(start + 8 - KERNEL + 1, count), :]
        for k in range(1, KERNEL):
            v = v + taps(k) * xs[l, pl.ds(start + 8 - KERNEL + 1 + k, count), :]
        return silu(v)

    for l in range(2):
        at = pl.ds(l * LANES, LANES)
        xs[l, 0:8, :] = sedge[:, at]
        xs[l, 8:8 + tokens, :] = si_ref[:, at].astype(F32)
    b_conv = conv(0, lambda k: cs_ref[k:k + 1, 0:LANES], 0, tokens).astype(BF16)
    c_conv = conv(1, lambda k: cs_ref[k:k + 1, LANES:2 * LANES], 0, tokens).astype(BF16)
    b_t = b_conv.astype(F32).T.astype(BF16)
    bt[...] = b_t
    cc[...] = c_conv
    for b in range(blocks):
        lo = b * SPAN
        sc = dot(c_conv[lo:lo + SPAN], b_t[:, lo:lo + SPAN])
        scores[b] = jnp.where(lower, sc, 0.0)

    for i in range(1, n_head):
        param_copies(peer(i), peer(i), i)[1].wait_recv()

    def spreader(g):
        return spread_matrix(g * per, width)

    def state_copies(dst, slot, k, j):
        return (
            pltpu.make_async_remote_copy(
                s_out.at[dst, j], slots.at[slot, j], s_ss.at[k, j], s_rs.at[slot, j],
                device_id=at_head(dst), device_id_type=MESH),
            pltpu.make_async_remote_copy(
                dx.at[dst, j], d_slots.at[slot, j], d_ss.at[k, j], d_rs.at[slot, j],
                device_id=at_head(dst), device_id_type=MESH),
        )

    def form(q, j, slot):
        g = q * pieces + j
        base = pl.multiple_of(g * GROUP, GROUP)
        jb = pl.multiple_of(j * GROUP, GROUP)
        spread = spreader(g)
        sb = dot(step_hl[...], spread)
        wb = dot(w_hl[...], spread)
        for l in range(2):
            at = pl.ds(pl.multiple_of(base + l * LANES, LANES), LANES)
            tap_at = pl.ds(pl.multiple_of(jb + l * LANES, LANES), LANES)
            half = slice(l * LANES, (l + 1) * LANES)
            xs[2 * slot + l, 0:8, :] = edge[:, at]
            for r in range(0, tokens, CHUNK):
                xs[2 * slot + l, 8 + r:8 + r + CHUNK, :] = x_ref[r:r + CHUNK, at].astype(F32)
            taps = [jnp.broadcast_to(cwb[q, k:k + 1, tap_at], (8, LANES)) for k in range(KERNEL + 1)]
            taps = [jnp.tile(t, (CHUNK // 8, 1)) for t in taps]
            for r in range(0, tokens, CHUNK):
                xv = conv(2 * slot + l, lambda k: taps[k], r, CHUNK).astype(BF16)
                xc[r:r + CHUNK, at] = xv
                u = (xv.astype(F32) * sb[r:r + CHUNK, half]).astype(BF16)
                uv[r:r + CHUNK, at] = u
                uw[slot, r:r + CHUNK, half] = (
                    u.astype(F32) * wb[r:r + CHUNK, half]).astype(BF16)
        d = dot(dec_hl[...], spread)[0:8]
        dx[q, j] = d
        first = dot(bt[:, 0:SPAN], uw[slot, 0:SPAN, :])
        second = dot(bt[:, SPAN:2 * SPAN], uw[slot, SPAN:2 * SPAN, :])
        s0[q, j] = first.astype(BF16)
        return d, (d[1:2] * first + second).astype(BF16)

    def send(i, j):
        for copy in state_copies(peer(i), me, i, j):
            copy.start()

    def form_piece(j):
        made = [form(peer(i), j, i % 2) for i in (1, 2)]
        for i in (1, 2):
            s_out[peer(i), j] = made[i - 1][1]
        for i in (1, 2):
            send(i, j)
        far = [form(peer(i), j, i % 2) for i in range(3, n_head)]
        d, mine = form(me, j, 0)
        for i in range(3, n_head):
            s_out[peer(i), j] = far[i - 3][1]
        slots[me, j] = mine
        d_slots[me, j] = d
        for i in range(3, n_head):
            send(i, j)

    lane = lax.broadcasted_iota(jnp.int32, (1, LANES), 1)

    def local(g):
        base = pl.multiple_of(g * GROUP, GROUP)
        q = g // pieces
        j = lax.rem(g, pieces)
        for b in range(blocks):
            lo = b * SPAN
            turned = pltpu.roll(cum[lo:lo + SPAN, :], lax.rem(LANES - g * per, LANES), 1)
            for l in range(2):
                at = pl.ds(pl.multiple_of(base + l * LANES, LANES), LANES)
                u = uv[lo:lo + SPAN, at]
                spot = 2 * b + l
                for k in range(2):
                    h = l * 2 + k
                    row = cum_t[pl.ds(g * per + h, 1), lo:lo + SPAN]
                    for r in range(0, SPAN, CHUNK):
                        col = jnp.broadcast_to(turned[r:r + CHUNK, h:h + 1], (CHUNK, LANES))
                        to = slice(k * SPAN + r, k * SPAN + r + CHUNK)
                        for s in range(0, r + 1, LANES):
                            gap = col - row[:, s:s + LANES]
                            if s + LANES > r:
                                gap = jnp.minimum(gap, 0.0)
                            mix[spot, to, s:s + LANES] = (
                                jnp.exp2(gap) * scores[b, r:r + CHUNK, s:s + LANES]).astype(BF16)
                made = dot(mix[spot], u)
                local_terms = jnp.where(lane < width, made[0:SPAN], made[SPAN:2 * SPAN])
                skip = dx[q, j, 3:4, l * LANES:(l + 1) * LANES]
                acc[lo:lo + SPAN, at] = (
                    local_terms + skip * xc[lo:lo + SPAN, at].astype(F32)).astype(BF16)
        acc_copy(g).start()

    def acc_copy(g):
        at = pl.ds(pl.multiple_of(g * GROUP, GROUP), GROUP)
        return pltpu.make_async_copy(acc.at[:, at], acc_hbm.at[:, at], acc_sem.at[g])

    def chain_copy(j):
        return pltpu.make_async_remote_copy(
            ch_out.at[j], ch_in.at[j], ch_ss.at[j], ch_rs.at[j],
            device_id=(run, up, me), device_id_type=MESH)

    def back_copy(dst, slot, k, j):
        return pltpu.make_async_remote_copy(
            p_out.at[dst, j], inc.at[slot, j], p_ss.at[k, j], p_rs.at[slot, j],
            device_id=at_head(dst), device_id_type=MESH)

    def own_copy(j):
        return pltpu.make_async_copy(p_out.at[me, j], inc.at[me, j], own_sem.at[j])

    def chain_piece(j):
        for i in range(1, n_head):
            for copy in state_copies(peer(i), peer(i), i, j):
                copy.wait_recv()
        q_sum = slots[0, j].astype(F32)
        r = d_slots[0, j, 2:3]
        for e in range(1, n_head):
            d = d_slots[e, j, 2:3]
            q_sum = d * q_sum + slots[e, j].astype(F32)
            r = d * r

        @pl.when(c > 0)
        def _():
            chain_copy(j).wait_recv()

        @pl.when(c == 0)
        def _():
            ch_in[j] = jnp.zeros((state, GROUP), BF16)

        arriving = ch_in[j].astype(F32)
        ch_out[j] = (r * arriving + q_sum).astype(BF16)

        @pl.when(c < n_ctx - 1)
        def _():
            chain_copy(j).start()

        prefix = arriving
        p_out[0, j] = prefix.astype(BF16)
        for e in range(1, n_head):
            prefix = d_slots[e - 1, j, 2:3] * prefix + slots[e - 1, j].astype(F32)
            p_out[e, j] = prefix.astype(BF16)
        for i in range(1, n_head):
            back_copy(peer(i), me, i, j).start()
        own_copy(j).start()

    units = n_head * pieces
    every = 3
    turns = pieces + (units - 1) // every + 1
    lag = jnp.minimum(c, turns - 1 - pieces)

    def chain_turn(turn):
        p = turn - 1 - lag

        @pl.when(jnp.logical_and(p >= 0, p < pieces))
        def _():
            chain_piece(p)

    for q in range(n_head):
        x_copy(q).wait()

    def form_turn(j, carry):
        form_piece(j)
        chain_turn(j)
        return carry

    lax.fori_loop(0, pieces, form_turn, 0)
    s0_copy = pltpu.make_async_copy(s0, s0_hbm, s0_sem)
    s0_copy.start()

    for spot in range(4):
        for k in range(2):
            mix[spot, k * SPAN:k * SPAN + LANES, LANES:] = jnp.zeros((LANES, SPAN - LANES), BF16)

    def local_turn(u, carry):
        local(u)

        @pl.when(lax.rem(u, every) == 0)
        def _():
            chain_turn(pieces + u // every)
        return carry

    lax.fori_loop(0, units, local_turn, 0)

    edge_copy.wait_send()
    for i in range(1, n_head):
        for copy in param_copies(peer(i), me, i):
            copy.wait_send()

    def drain(j, carry):
        for i in range(1, n_head):
            for copy in state_copies(peer(i), me, i, j):
                copy.wait_send()
            back_copy(peer(i), me, i, j).wait_send()

            back_copy(peer(i), peer(i), i, j).wait_recv()
        own_copy(j).wait()

        @pl.when(c < n_ctx - 1)
        def _():
            chain_copy(j).wait_send()
        return carry

    lax.fori_loop(0, pieces, drain, 0)
    s0_copy.wait()

    def drain_acc(g, carry):
        acc_copy(g).wait()
        return carry

    lax.fori_loop(0, units, drain_acc, 0)


def finish(width, acc_ref, inc_ref, s0_ref, dx_ref, ec_ref, cc_ref, out_ref):
    q = pl.program_id(0)
    pieces = inc_ref.shape[1]
    per = GROUP // width
    for j in range(pieces):
        spread = spread_matrix((q * pieces + j) * per, width)
        entering = inc_ref[0, j]
        middle = (dx_ref[0, j, 0:1] * entering.astype(F32) + s0_ref[0, j].astype(F32)).astype(BF16)
        at = slice(j * GROUP, (j + 1) * GROUP)
        for b, held in enumerate((entering, middle)):
            rows = slice(b * SPAN, (b + 1) * SPAN)
            carried = dot(ec_ref[rows, :], spread) * dot(cc_ref[rows, :], held)
            out_ref[rows, at] = (acc_ref[rows, at].astype(F32) + carried).astype(BF16)


def per_device(n_ctx, n_head, inner_tokens, state_inputs, step_raw, conv_inner, conv_state, head_rates, skip_gain):
    tokens, channels = inner_tokens.shape
    heads = step_raw.shape[1]
    width = channels // heads
    state = state_inputs.shape[1] // 2
    pieces = channels // n_head // GROUP
    part = channels // n_head
    vm = pltpu.VMEM
    dma = pltpu.SemaphoreType.DMA
    grid4 = (n_head, pieces, state, GROUP)
    small4 = (n_head, pieces, 8, GROUP)
    scratch = [
        vm((tokens, channels), BF16), vm((16, channels), BF16),
        vm((n_head, 8, part), F32), vm((n_head, 8, LANES), F32),
        vm((16, channels // 5), F32), vm((16, channels // 5), BF16), vm((16, channels // 5), BF16),
        vm((8, channels), F32), vm((8, 2 * state), F32), vm((4, tokens + 8, LANES), F32),
        vm((tokens, LANES), F32), vm((LANES, tokens), F32),
        vm((tokens, 2 * LANES), BF16), vm((tokens, 2 * LANES), BF16),
        vm((16, 2 * LANES), BF16),
        vm((tokens // SPAN, SPAN, SPAN), F32), vm((state, tokens), BF16),
        vm((tokens, channels), BF16), vm((tokens, channels), BF16),
        vm((2, tokens, GROUP), BF16), vm((4, 2 * SPAN, SPAN), BF16), vm((tokens, channels), BF16),
        vm(grid4, BF16), vm(grid4, BF16), vm(grid4, BF16), vm(small4, F32),
        vm((pieces, state, GROUP), BF16), vm((pieces, state, GROUP), BF16),
        vm(grid4, BF16),
        dma((n_head,)), dma((n_head,)), dma((n_head,)), dma((n_head,)),
        dma, dma,
        dma((n_head, pieces)), dma((n_head, pieces)), dma((n_head, pieces)), dma((n_head, pieces)),
        dma((pieces,)), dma((pieces,)),
        dma((n_head, pieces)), dma((n_head, pieces)),
        dma((n_head,)), dma, dma((n_head * pieces,)), dma, dma((pieces,)),
    ]
    in_vmem = pl.BlockSpec(memory_space=pltpu.VMEM)
    anywhere = pl.BlockSpec(memory_space=pl.ANY)
    shape = jax.ShapeDtypeStruct
    parts = pl.pallas_call(
        functools.partial(kernel, n_ctx, n_head, heads, width, pieces),
        out_shape=(
            shape((tokens, channels), BF16), shape(grid4, BF16), shape(grid4, BF16),
            shape(small4, F32), shape((tokens, 2 * LANES), BF16), shape((tokens, state), BF16),
        ),
        in_specs=[anywhere] + [in_vmem] * 6,
        out_specs=(anywhere, anywhere, anywhere, in_vmem, in_vmem, in_vmem),
        scratch_shapes=scratch,
        compiler_params=pltpu.CompilerParams(
            collective_id=0, has_side_effects=True, vmem_limit_bytes=56 * 1024 * 1024
        ),
        name="ssd_layer",
    )(inner_tokens, state_inputs, step_raw.T, conv_inner, conv_state, head_rates, skip_gain[None])
    column = pl.BlockSpec((tokens, part), lambda q: (0, q))
    states = pl.BlockSpec((1, pieces, state, GROUP), lambda q: (q, 0, 0, 0))
    return pl.pallas_call(
        functools.partial(finish, width),
        grid=(n_head,),
        out_shape=shape((tokens, channels), BF16),
        in_specs=[
            column, states, states,
            pl.BlockSpec((1, pieces, 8, GROUP), lambda q: (q, 0, 0, 0)),
            pl.BlockSpec((tokens, 2 * LANES), lambda q: (0, 0)),
            pl.BlockSpec((tokens, state), lambda q: (0, 0)),
        ],
        out_specs=column,
        compiler_params=pltpu.CompilerParams(vmem_limit_bytes=56 * 1024 * 1024),
        name="carried_terms",
    )(*parts)


def solution(mesh):
    return jax.shard_map(
        functools.partial(per_device, mesh.shape["ctx"], mesh.shape["head"]),
        mesh=mesh,
        in_specs=(
            P(("run", "ctx", "head"), None),
            P(("run", "ctx", "head"), None),
            P(("run", "ctx", "head"), None),
            P(None, "head"),
            P(),
            P("run", "head"),
            P("head"),
        ),
        out_specs=P(("run", "ctx", "head"), None),
        check_vma=False,
    )
```

```python
import functools

import jax
import jax.numpy as jnp
from jax import lax
from jax.experimental import pallas as pl
from jax.experimental.pallas import tpu as pltpu
from jax.sharding import PartitionSpec as P

KERNEL = 4
SPAN = 256
GROUP = 256
LANES = 128
LOG2E = 1.4426950408889634
F32 = jnp.float32
BF16 = jnp.bfloat16
MESH = pl.DeviceIdType.MESH


def dot(a, b):
    return jnp.dot(a, b, preferred_element_type=F32)


def split2(v):
    hi = v.astype(BF16)
    lo = (v - hi.astype(F32)).astype(BF16)
    return jnp.concatenate([hi, lo], axis=1)


def silu(v):
    return v * (0.5 + 0.5 * jnp.tanh(0.5 * v))


def softplus(v):
    return jnp.maximum(v, 0.0) + jnp.log(1.0 + jnp.exp(-jnp.abs(v)))


def spread_matrix(first, width):
    k = lax.broadcasted_iota(jnp.int32, (LANES, GROUP), 0)
    l = lax.broadcasted_iota(jnp.int32, (LANES, GROUP), 1)
    place = k - jnp.right_shift(l, width.bit_length() - 1)
    once = jnp.where(place == first, 1.0, 0.0).astype(BF16)
    return jnp.concatenate([once, once], axis=0)


def kernel(
    n_ctx, n_head, heads, width, pieces,
    x_hbm, si_ref, sr_ref, cw_ref, cs_ref, hr_ref, sg_ref,
    acc_hbm, inc, s0_hbm, dx, ec_hl, cc,
    x_ref, tail_v, cwb, smb, eb32, ebs, ebr, edge, sedge, xs,
    cum, cum_t, step_hl, w_hl, dec_hl, scores, bt,
    xc, uv, acc, s0, s_out, slots, d_slots, ch_in, ch_out, p_out,
    cw_ss, cw_rs, sm_ss, sm_rs, eb_ss, eb_rs, s_ss, s_rs, d_ss, d_rs, ch_ss, ch_rs, p_ss, p_rs,
    x_sem, tail_sem, acc_sem, s0_sem, own_sem,
):
    tokens, channels = x_ref.shape
    blocks = tokens // SPAN
    per = GROUP // width
    state = cc.shape[1]
    run = lax.axis_index("run")
    c = lax.axis_index("ctx")
    me = lax.axis_index("head")
    flat = c * n_head + me
    total = n_ctx * n_head
    nxt = lax.rem(flat + 1, total)
    prv = lax.rem(flat + total - 1, total)
    up = lax.rem(c + 1, n_ctx)
    down = lax.rem(c + n_ctx - 1, n_ctx)

    def peer(i):
        return lax.rem(me + i, n_head)

    def at_head(h):
        return (run, c, h)

    def x_copy(q):
        at = pl.ds(pl.multiple_of(q * pieces * GROUP, GROUP), pieces * GROUP)
        return pltpu.make_async_copy(x_hbm.at[:, at], x_ref.at[:, at], x_sem.at[q])

    tail_copy = pltpu.make_async_copy(x_hbm.at[pl.ds(tokens - 16, 16)], tail_v, tail_sem)
    tail_copy.start()
    for q in range(n_head):
        x_copy(q).start()

    barrier = pltpu.get_barrier_semaphore()
    for i in range(1, n_head):
        pl.semaphore_signal(barrier, inc=1, device_id=at_head(peer(i)), device_id_type=MESH)
    for f in (nxt, prv):
        pl.semaphore_signal(
            barrier, inc=1, device_id=(run, f // n_head, lax.rem(f, n_head)), device_id_type=MESH
        )
    for z in (up, down):
        pl.semaphore_signal(barrier, inc=1, device_id=(run, z, me), device_id_type=MESH)

    part = channels // 5
    tail_copy.wait()
    tail = tail_v[...].astype(F32)
    stail = si_ref[tokens - 16:, :].astype(F32)
    eb32[...] = jnp.zeros_like(eb32)
    for i in range(5):
        eb32[3 * i:3 * i + 3, :] = tail[13:16, i * part:(i + 1) * part]
    for r in range(3):
        eb32[15:16, r * 2 * state:(r + 1) * 2 * state] = stail[13 + r:14 + r, :]
    ebs[...] = eb32[...].astype(BF16)
    cwb[me, 0:KERNEL + 1, :] = cw_ref[...]
    cwb[me, KERNEL + 1:8, :] = jnp.zeros((8 - KERNEL - 1, cw_ref.shape[1]), F32)
    own = heads // n_head
    smb[me] = jnp.zeros((8, LANES), F32)
    smb[me, 0:2, 0:own] = hr_ref[...]
    smb[me, 2:3, 0:own] = sg_ref[...]
    smb[me] = pltpu.roll(smb[me], me * own, 1)

    pl.semaphore_wait(barrier, n_head - 1 + 4)

    edge_copy = pltpu.make_async_remote_copy(
        ebs, ebr, eb_ss, eb_rs, device_id=(run, nxt // n_head, lax.rem(nxt, n_head)), device_id_type=MESH
    )
    edge_copy.start()

    def param_copies(dst, slot, k):
        return (
            pltpu.make_async_remote_copy(
                smb.at[slot], smb.at[slot], sm_ss.at[k], sm_rs.at[slot],
                device_id=at_head(dst), device_id_type=MESH),
            pltpu.make_async_remote_copy(
                cwb.at[slot], cwb.at[slot], cw_ss.at[k], cw_rs.at[slot],
                device_id=at_head(dst), device_id_type=MESH),
        )

    for i in range(1, n_head):
        for copy in param_copies(peer(i), me, i):
            copy.start()
    for i in range(1, n_head):
        param_copies(peer(i), peer(i), i)[0].wait_recv()

    small = jnp.sum(smb[...], axis=0)
    bias = small[0:1]
    rate = jnp.exp(small[1:2])
    gain = small[2:3]
    raw = jnp.concatenate(
        [sr_ref[...].astype(F32), jnp.zeros((LANES - heads, tokens), F32)], axis=0
    ).T
    step = softplus(raw + bias)
    decay = -step * rate
    rows = lax.broadcasted_iota(jnp.int32, (SPAN, SPAN), 0)
    cols = lax.broadcasted_iota(jnp.int32, (SPAN, SPAN), 1)
    lower = rows >= cols
    tri = jnp.where(lower, 1.0, 0.0).astype(F32)
    step_hl[...] = split2(step)
    ends = []
    for b in range(blocks):
        lo = b * SPAN
        cm = jnp.dot(tri, decay[lo:lo + SPAN] * LOG2E, precision=lax.Precision.HIGHEST,
                     preferred_element_type=F32)
        cum[lo:lo + SPAN, :] = cm
        cum_t[:, lo:lo + SPAN] = cm.T
        end = cm[SPAN - 1:SPAN]
        w_hl[lo:lo + SPAN, :] = split2(jnp.exp2(end - cm))
        ec_hl[lo:lo + SPAN, :] = split2(jnp.exp2(cm))
        ends.append(end)
    dec_rows = jnp.concatenate(
        [jnp.exp2(ends[0]), jnp.exp2(ends[1]), jnp.exp2(ends[0] + ends[1]), gain,
         jnp.zeros((12, LANES), F32)], axis=0)
    dec_hl[...] = split2(dec_rows)
    d_slots[me] = split2(dec_rows)

    def decay_copy(dst, slot, k):
        return pltpu.make_async_remote_copy(
            d_slots.at[slot], d_slots.at[slot], d_ss.at[k], d_rs.at[slot],
            device_id=at_head(dst), device_id_type=MESH)

    for i in range(1, n_head):
        decay_copy(peer(i), me, i).start()

    edge_copy.wait_recv()
    eb32[...] = jnp.where(flat == 0, 0.0, ebr[...].astype(F32))
    for i in range(5):
        edge[5:8, i * part:(i + 1) * part] = eb32[3 * i:3 * i + 3, :]
    for r in range(3):
        sedge[5 + r:6 + r, :] = eb32[15:16, r * 2 * state:(r + 1) * 2 * state]

    def conv(l, taps):
        v = taps(KERNEL) + taps(0) * xs[l, pl.ds(8 - KERNEL + 1, tokens), :]
        for k in range(1, KERNEL):
            v = v + taps(k) * xs[l, pl.ds(8 - KERNEL + 1 + k, tokens), :]
        return silu(v).astype(BF16)

    for l in range(2):
        at = pl.ds(l * LANES, LANES)
        xs[l, 0:8, :] = sedge[:, at]
        xs[l, 8:8 + tokens, :] = si_ref[:, at].astype(F32)
    b_conv = conv(0, lambda k: cs_ref[k:k + 1, 0:LANES])
    c_conv = conv(1, lambda k: cs_ref[k:k + 1, LANES:2 * LANES])
    b_t = b_conv.astype(F32).T.astype(BF16)
    bt[...] = b_t
    cc[...] = c_conv
    for b in range(blocks):
        lo = b * SPAN
        sc = dot(c_conv[lo:lo + SPAN], b_t[:, lo:lo + SPAN])
        scores[b] = jnp.where(lower, sc, 0.0)

    for i in range(1, n_head):
        param_copies(peer(i), peer(i), i)[1].wait_recv()

    def spreader(g):
        return spread_matrix(g * per, width)

    def state_copy(dst, slot, k, j):
        return pltpu.make_async_remote_copy(
            s_out.at[dst, j], slots.at[slot, j], s_ss.at[k, j], s_rs.at[slot, j],
            device_id=at_head(dst), device_id_type=MESH)

    def form(q, j, slot):
        g = q * pieces + j
        base = pl.multiple_of(g * GROUP, GROUP)
        jb = pl.multiple_of(j * GROUP, GROUP)
        spread = spreader(g)
        us = []
        sb = dot(step_hl[...], spread)
        wb = dot(w_hl[...], spread)
        for l in range(2):
            at = pl.ds(pl.multiple_of(base + l * LANES, LANES), LANES)
            tap_at = pl.ds(pl.multiple_of(jb + l * LANES, LANES), LANES)
            xs[2 * slot + l, 0:8, :] = edge[:, at]
            xs[2 * slot + l, 8:8 + tokens, :] = x_ref[:, at].astype(F32)
            xv = conv(2 * slot + l, lambda k: cwb[q, k:k + 1, tap_at])
            xc[:, at] = xv
            half = slice(l * LANES, (l + 1) * LANES)
            u = (xv.astype(F32) * sb[:, half]).astype(BF16)
            uv[:, at] = u
            us.append((u.astype(F32) * wb[:, half]).astype(BF16))
        uw = jnp.concatenate(us, axis=1)
        d = dot(dec_hl[...], spread)[0:8]
        dx[q, j] = d
        first = dot(bt[:, 0:SPAN], uw[0:SPAN])
        second = dot(bt[:, SPAN:2 * SPAN], uw[SPAN:2 * SPAN])
        s0[q, j] = first.astype(BF16)
        return d, (d[1:2] * first + second).astype(BF16)

    def send(i, j):
        state_copy(peer(i), me, i, j).start()

    def form_piece(j):
        made = [form(peer(i), j, i % 2) for i in (1, 2)]
        for i in (1, 2):
            s_out[peer(i), j] = made[i - 1][1]
        for i in (1, 2):
            send(i, j)
        far = [form(peer(i), j, i % 2) for i in range(3, n_head)]
        mine = form(me, j, 0)[1]
        for i in range(3, n_head):
            s_out[peer(i), j] = far[i - 3][1]
        slots[me, j] = mine
        for i in range(3, n_head):
            send(i, j)

    lane = lax.broadcasted_iota(jnp.int32, (1, LANES), 1)

    def local(g):
        base = pl.multiple_of(g * GROUP, GROUP)
        q = g // pieces
        j = lax.rem(g, pieces)
        half = SPAN // 2
        for b in range(blocks):
            lo = b * SPAN
            turned = pltpu.roll(cum[lo:lo + SPAN, :], lax.rem(LANES - g * per, LANES), 1)
            for l in range(2):
                at = pl.ds(pl.multiple_of(base + l * LANES, LANES), LANES)
                u = uv[lo:lo + SPAN, at]
                mixing = []
                for k in range(2):
                    h = l * 2 + k
                    col = turned[:, h:h + 1]
                    row = cum_t[pl.ds(g * per + h, 1), lo:lo + SPAN]
                    top = jnp.exp2(jnp.minimum(col[0:half] - row[:, 0:half], 0.0))
                    low = jnp.exp2(jnp.minimum(col[half:SPAN] - row, 0.0))
                    top = (top * scores[b, 0:half, 0:half]).astype(BF16)
                    low = (low * scores[b, half:SPAN, :]).astype(BF16)
                    mixing += [jnp.concatenate([top, jnp.zeros_like(top)], axis=1), low]
                made = dot(jnp.concatenate(mixing, axis=0), u)
                local_terms = jnp.where(lane < width, made[0:SPAN], made[SPAN:2 * SPAN])
                skip = dx[q, j, 3:4, l * LANES:(l + 1) * LANES]
                acc[lo:lo + SPAN, at] = (
                    local_terms + skip * xc[lo:lo + SPAN, at].astype(F32)).astype(BF16)
        acc_copy(g).start()

    def acc_copy(g):
        at = pl.ds(pl.multiple_of(g * GROUP, GROUP), GROUP)
        return pltpu.make_async_copy(acc.at[:, at], acc_hbm.at[:, at], acc_sem.at[g])

    def chain_copy(j):
        return pltpu.make_async_remote_copy(
            ch_out.at[j], ch_in.at[j], ch_ss.at[j], ch_rs.at[j],
            device_id=(run, up, me), device_id_type=MESH)

    def back_copy(dst, slot, k, j):
        return pltpu.make_async_remote_copy(
            p_out.at[dst, j], inc.at[slot, j], p_ss.at[k, j], p_rs.at[slot, j],
            device_id=at_head(dst), device_id_type=MESH)

    def own_copy(j):
        return pltpu.make_async_copy(p_out.at[me, j], inc.at[me, j], own_sem.at[j])

    def chain_piece(j):
        for i in range(1, n_head):
            state_copy(peer(i), peer(i), i, j).wait_recv()
        spread = spreader(me * pieces + j)
        ds = [dot(d_slots[e], spread)[2:3] for e in range(n_head)]
        q_sum = slots[0, j].astype(F32)
        r = ds[0]
        for e in range(1, n_head):
            q_sum = ds[e] * q_sum + slots[e, j].astype(F32)
            r = ds[e] * r

        @pl.when(c > 0)
        def _():
            chain_copy(j).wait_recv()

        @pl.when(c == 0)
        def _():
            ch_in[j] = jnp.zeros((state, GROUP), BF16)

        arriving = ch_in[j].astype(F32)
        ch_out[j] = (r * arriving + q_sum).astype(BF16)

        @pl.when(c < n_ctx - 1)
        def _():
            chain_copy(j).start()

        prefix = arriving
        p_out[0, j] = prefix.astype(BF16)
        for e in range(1, n_head):
            prefix = ds[e - 1] * prefix + slots[e - 1, j].astype(F32)
            p_out[e, j] = prefix.astype(BF16)
        for i in range(1, n_head):
            back_copy(peer(i), me, i, j).start()
        own_copy(j).start()

    units = n_head * pieces
    every = 2
    turns = pieces + (units - 1) // every + 1
    lag = jnp.minimum(c + 3, turns - 1 - pieces)

    def chain_turn(turn):
        p = turn - 1 - lag

        @pl.when(jnp.logical_and(p >= 0, p < pieces))
        def _():
            chain_piece(p)

    for q in range(n_head):
        x_copy(q).wait()
    for i in range(1, n_head):
        decay_copy(peer(i), peer(i), i).wait_recv()

    def form_turn(j, carry):
        form_piece(j)
        chain_turn(j)
        return carry

    lax.fori_loop(0, pieces, form_turn, 0)
    s0_copy = pltpu.make_async_copy(s0, s0_hbm, s0_sem)
    s0_copy.start()

    def local_turn(u, carry):
        local(u)

        @pl.when(lax.rem(u, every) == 0)
        def _():
            chain_turn(pieces + u // every)
        return carry

    lax.fori_loop(0, units, local_turn, 0)

    edge_copy.wait_send()
    for i in range(1, n_head):
        for copy in param_copies(peer(i), me, i):
            copy.wait_send()

    for i in range(1, n_head):
        decay_copy(peer(i), me, i).wait_send()

    def drain(j, carry):
        for i in range(1, n_head):
            state_copy(peer(i), me, i, j).wait_send()
            back_copy(peer(i), me, i, j).wait_send()

            back_copy(peer(i), peer(i), i, j).wait_recv()
        own_copy(j).wait()

        @pl.when(c < n_ctx - 1)
        def _():
            chain_copy(j).wait_send()
        return carry

    lax.fori_loop(0, pieces, drain, 0)
    s0_copy.wait()

    def drain_acc(g, carry):
        acc_copy(g).wait()
        return carry

    lax.fori_loop(0, units, drain_acc, 0)


def finish(width, acc_ref, inc_ref, s0_ref, dx_ref, ec_ref, cc_ref, out_ref):
    q = pl.program_id(0)
    pieces = inc_ref.shape[1]
    per = GROUP // width
    for j in range(pieces):
        spread = spread_matrix((q * pieces + j) * per, width)
        entering = inc_ref[0, j]
        middle = (dx_ref[0, j, 0:1] * entering.astype(F32) + s0_ref[0, j].astype(F32)).astype(BF16)
        at = slice(j * GROUP, (j + 1) * GROUP)
        for b, held in enumerate((entering, middle)):
            rows = slice(b * SPAN, (b + 1) * SPAN)
            carried = dot(ec_ref[rows, :], spread) * dot(cc_ref[rows, :], held)
            out_ref[rows, at] = (acc_ref[rows, at].astype(F32) + carried).astype(BF16)


def per_device(n_ctx, n_head, inner_tokens, state_inputs, step_raw, conv_inner, conv_state, head_rates, skip_gain):
    tokens, channels = inner_tokens.shape
    heads = step_raw.shape[1]
    width = channels // heads
    state = state_inputs.shape[1] // 2
    pieces = channels // n_head // GROUP
    part = channels // n_head
    vm = pltpu.VMEM
    dma = pltpu.SemaphoreType.DMA
    grid4 = (n_head, pieces, state, GROUP)
    small4 = (n_head, pieces, 8, GROUP)
    scratch = [
        vm((tokens, channels), BF16), vm((16, channels), BF16),
        vm((n_head, 8, part), F32), vm((n_head, 8, LANES), F32),
        vm((16, channels // 5), F32), vm((16, channels // 5), BF16), vm((16, channels // 5), BF16),
        vm((8, channels), F32), vm((8, 2 * state), F32), vm((4, tokens + 8, LANES), F32),
        vm((tokens, LANES), F32), vm((LANES, tokens), F32),
        vm((tokens, 2 * LANES), BF16), vm((tokens, 2 * LANES), BF16),
        vm((16, 2 * LANES), BF16),
        vm((tokens // SPAN, SPAN, SPAN), F32), vm((state, tokens), BF16),
        vm((tokens, channels), BF16), vm((tokens, channels), BF16), vm((tokens, channels), BF16),
        vm(grid4, BF16), vm(grid4, BF16), vm(grid4, BF16), vm((n_head, 16, 2 * LANES), BF16),
        vm((pieces, state, GROUP), BF16), vm((pieces, state, GROUP), BF16),
        vm(grid4, BF16),
        dma((n_head,)), dma((n_head,)), dma((n_head,)), dma((n_head,)),
        dma, dma,
        dma((n_head, pieces)), dma((n_head, pieces)), dma((n_head,)), dma((n_head,)),
        dma((pieces,)), dma((pieces,)),
        dma((n_head, pieces)), dma((n_head, pieces)),
        dma((n_head,)), dma, dma((n_head * pieces,)), dma, dma((pieces,)),
    ]
    in_vmem = pl.BlockSpec(memory_space=pltpu.VMEM)
    anywhere = pl.BlockSpec(memory_space=pl.ANY)
    shape = jax.ShapeDtypeStruct
    parts = pl.pallas_call(
        functools.partial(kernel, n_ctx, n_head, heads, width, pieces),
        out_shape=(
            shape((tokens, channels), BF16), shape(grid4, BF16), shape(grid4, BF16),
            shape(small4, F32), shape((tokens, 2 * LANES), BF16), shape((tokens, state), BF16),
        ),
        in_specs=[anywhere] + [in_vmem] * 6,
        out_specs=(anywhere, anywhere, anywhere, in_vmem, in_vmem, in_vmem),
        scratch_shapes=scratch,
        compiler_params=pltpu.CompilerParams(
            collective_id=0, has_side_effects=True, vmem_limit_bytes=56 * 1024 * 1024
        ),
        name="ssd_layer",
    )(inner_tokens, state_inputs, step_raw.T, conv_inner, conv_state, head_rates, skip_gain[None])
    column = pl.BlockSpec((tokens, part), lambda q: (0, q))
    states = pl.BlockSpec((1, pieces, state, GROUP), lambda q: (q, 0, 0, 0))
    return pl.pallas_call(
        functools.partial(finish, width),
        grid=(n_head,),
        out_shape=shape((tokens, channels), BF16),
        in_specs=[
            column, states, states,
            pl.BlockSpec((1, pieces, 8, GROUP), lambda q: (q, 0, 0, 0)),
            pl.BlockSpec((tokens, 2 * LANES), lambda q: (0, 0)),
            pl.BlockSpec((tokens, state), lambda q: (0, 0)),
        ],
        out_specs=column,
        compiler_params=pltpu.CompilerParams(vmem_limit_bytes=56 * 1024 * 1024),
        name="carried_terms",
    )(*parts)


def solution(mesh):
    return jax.shard_map(
        functools.partial(per_device, mesh.shape["ctx"], mesh.shape["head"]),
        mesh=mesh,
        in_specs=(
            P(("run", "ctx", "head"), None),
            P(("run", "ctx", "head"), None),
            P(("run", "ctx", "head"), None),
            P(None, "head"),
            P(),
            P("run", "head"),
            P("head"),
        ),
        out_specs=P(("run", "ctx", "head"), None),
        check_vma=False,
    )
```
